32 devices in a mesh: dp: 8 (over y, x, core), tensor: 4 (over z).
Axes of the slice: x: 2, y: 2, z: 4, core: 2. Of those that a mesh axis runs over, the one named last changes fastest.
Arguments:
- tokens: bfloat16 [8192, 2048], P('dp', 'tensor'), may hold values from -6 to 6
- lengths: int32 [8], P('dp'), may hold values from 256 to 1024, as said below
- cotangent: bfloat16 [8192, 2048], P('dp', 'tensor'), may hold values from -6 to 6
- first_gain: float32 [2048], replicated, may hold values from 0.25 to 1.75
- query_weight: bfloat16 [2048, 2048], P(None, 'tensor'), may hold values from -0.125 to 0.125
- key_weight: bfloat16 [2048, 1024], P(None, 'tensor'), may hold values from -0.125 to 0.125
- value_weight: bfloat16 [2048, 1024], P(None, 'tensor'), may hold values from -0.125 to 0.125
- query_gain: float32 [128], replicated, may hold values from 0.25 to 1.75
- key_gain: float32 [128], replicated, may hold values from 0.25 to 1.75
- out_weight: bfloat16 [2048, 2048], P('tensor'), may hold values from -1.5 to 1.5
- second_gain: float32 [2048], replicated, may hold values from 0.25 to 1.75
- gate_weight: bfloat16 [2048, 6144], P(None, 'tensor'), may hold values from -0.125 to 0.125
- up_weight: bfloat16 [2048, 6144], P(None, 'tensor'), may hold values from -0.125 to 0.125
- down_weight: bfloat16 [6144, 2048], P('tensor'), may hold values from -0.078125 to 0.078125
Outputs:
- block_out: bfloat16 [8192, 2048], P('dp', 'tensor')
- token_grad: bfloat16 [8192, 2048], P('dp', 'tensor')
- first_gain_grad: float32 [2048], P('tensor')
- query_weight_grad: float32 [2048, 2048], P(None, 'tensor')
- key_weight_grad: float32 [2048, 1024], P(None, 'tensor')
- value_weight_grad: float32 [2048, 1024], P(None, 'tensor')
- query_gain_grad: float32 [128], replicated
- key_gain_grad: float32 [128], replicated
- out_weight_grad: float32 [2048, 2048], P('tensor')
- second_gain_grad: float32 [2048], P('tensor')
- gate_weight_grad: float32 [2048, 6144], P(None, 'tensor')
- up_weight_grad: float32 [2048, 6144], P(None, 'tensor')
- down_weight_grad: float32 [6144, 2048], P('tensor')
The draws below stay inside these ranges and needn't reach their ends.
Inputs may be any that keep to these rules, and one draw needn't show every extreme that they name: `lengths`: each sequence's number of valid tokens, all at its start; in every draw some sequence has exactly 1024.
All inputs are finite; a program needn't handle non-finite values.
Results may differ from the reference program's by a relative error of at most 0.024.
Values may be sent and summed in bfloat16 or wider, within the bound.
No kernel may reach another device: no remote copies, remote signals or barrier semaphores. Data moves between devices by JAX's collectives and lax.ppermute only.
A program may use at most 192 MiB of HBM per device.

```python
from functools import partial
import jax
import jax.numpy as jnp
from jax import lax

D = 2048
HEADS = 16
KV_HEADS = 8
HEAD_DIM = 128
FF = 6144
LEN = 1024
SEQS = 8
TOKENS = 8192


def draw_lengths(key, part):
    key_lens, key_full = jax.random.split(key)
    counts = jax.random.randint(key_lens, (SEQS,), LEN // 4, LEN + 1, dtype=jnp.int32)
    fullrow = jax.random.randint(key_full, (), 0, SEQS, dtype=jnp.int32)
    return jnp.where(jnp.arange(SEQS, dtype=jnp.int32) == fullrow, LEN, counts).astype(jnp.int32)


def shard_levels(key, extent, cuts, low, largest):
    def one(axis_at, parts):
        steps = jax.random.uniform(jax.random.fold_in(jax.random.fold_in(key, 6), axis_at), (parts,), jnp.float32, low / len(cuts), largest / len(cuts))
        return jnp.repeat(jnp.exp(steps), extent[axis_at] // parts).reshape((-1,) + (1,) * (len(extent) - axis_at - 1))

    level = one(*cuts[0])
    for cut in cuts[1:]:
        level = level * one(*cut)
    return level


def gaussian(rng, dims, spread, most, cuts=(), kind=jnp.bfloat16):
    values = spread * jax.random.normal(rng, dims, jnp.float32)
    if cuts:
        values = values * shard_levels(rng, dims, cuts, -0.22, 0.18)
    return jnp.clip(values, -most, most).astype(kind)


def setup_inputs(seed: int = 0) -> dict:
    streams_of = jax.random.split(jax.random.key(seed), 15)
    tokens = gaussian(streams_of[0], (TOKENS, D), 1.0, 6.0, ((0, 8), (1, 4)))
    lengths = draw_lengths(jax.random.fold_in(streams_of[14], 71), 0)
    cotangent = gaussian(streams_of[2], (TOKENS, D), 1.0, 6.0, ((0, 8), (1, 4)))
    first_gain = jnp.clip(1.0 + 0.15 * jax.random.normal(streams_of[3], (D,), jnp.float32), 0.25, 1.75)
    query_weight = gaussian(streams_of[4], (D, HEADS * HEAD_DIM), D ** -0.5, 0.125, ((1, 4),))
    key_weight = gaussian(streams_of[5], (D, KV_HEADS * HEAD_DIM), D ** -0.5, 0.125, ((1, 4),))
    value_weight = gaussian(streams_of[6], (D, KV_HEADS * HEAD_DIM), D ** -0.5, 0.125, ((1, 4),))
    query_gain = jnp.clip(1.0 + 0.15 * jax.random.normal(streams_of[7], (HEAD_DIM,), jnp.float32), 0.25, 1.75)
    key_gain = jnp.clip(1.0 + 0.15 * jax.random.normal(streams_of[8], (HEAD_DIM,), jnp.float32), 0.25, 1.75)
    out_weight = gaussian(streams_of[9], (HEADS * HEAD_DIM, D), (max(HEADS * HEAD_DIM * 8 // LEN, 1)) ** -0.5, 1.5, ((0, 4),))
    second_gain = jnp.clip(1.0 + 0.15 * jax.random.normal(streams_of[10], (D,), jnp.float32), 0.25, 1.75)
    gate_weight = gaussian(streams_of[11], (D, FF), D ** -0.5, 0.125, ((1, 4),))
    up_weight = gaussian(streams_of[12], (D, FF), D ** -0.5, 0.125, ((1, 4),))
    down_weight = gaussian(streams_of[13], (FF, D), FF ** -0.5, 0.078125, ((0, 4),))
    return {"tokens": tokens, "lengths": lengths, "cotangent": cotangent, "first_gain": first_gain, "query_weight": query_weight, "key_weight": key_weight, "value_weight": value_weight, "query_gain": query_gain, "key_gain": key_gain, "out_weight": out_weight, "second_gain": second_gain, "gate_weight": gate_weight, "up_weight": up_weight, "down_weight": down_weight}


@jax.custom_vjp
def low(v):
    return lax.optimization_barrier(v.astype(jnp.bfloat16)).astype(jnp.float32)

@jax.custom_vjp
def low_back(v):
    return v

def low_keep(v):
    return (low(v), None)

def low_pass(kept, grad):
    return (grad,)

def back_keep(v):
    return (v, None)

def back_low(kept, grad):
    return (low(grad),)
low.defvjp(low_keep, low_pass)
low_back.defvjp(back_keep, back_low)
EPSILON = 1e-06
ROPE_BASE = 1000000.0
HIGHEST = lax.Precision.HIGHEST

def matmul(left, right):
    return jnp.dot(left, right, precision=HIGHEST, preferred_element_type=jnp.float32)

def norm_rows(values, gain):
    factor = lax.rsqrt(lax.optimization_barrier(jnp.mean(values * values, axis=-1, keepdims=True)) + EPSILON)
    return values * factor * gain

def rope_tables(seq_len, head_dim):
    half_dim = head_dim // 2
    frequency = ROPE_BASE ** (-(jnp.arange(half_dim, dtype=jnp.float32) * 2.0 / head_dim))
    angles = jnp.arange(seq_len, dtype=jnp.float32)[:, None] * frequency[None, :]
    angles = jnp.concatenate([angles, angles], axis=1)
    return (jnp.cos(angles)[:, None, :], jnp.sin(angles)[:, None, :])

def rotate(values, cosine_table, sine_table):
    half_dim = values.shape[-1] // 2
    turned = jnp.concatenate([-values[..., half_dim:], values[..., :half_dim]], axis=-1)
    return values * cosine_table + turned * sine_table

def forward(length, tokens, first_gain, query_weight, key_weight, value_weight, query_gain, key_gain, out_weight, second_gain, gate_weight, up_weight, down_weight):
    normed = low(norm_rows(tokens, first_gain))
    queries = low_back(matmul(normed, query_weight)).reshape(LEN, HEADS, HEAD_DIM)
    key_rows = low_back(matmul(normed, key_weight)).reshape(LEN, KV_HEADS, HEAD_DIM)
    value_rows = low(low_back(matmul(normed, value_weight))).reshape(LEN, KV_HEADS, HEAD_DIM)
    cosine_table, sine_table = rope_tables(LEN, HEAD_DIM)
    queries = low(rotate(norm_rows(queries, query_gain), cosine_table, sine_table))
    key_rows = low(rotate(norm_rows(key_rows, key_gain), cosine_table, sine_table))
    group_size = HEADS // KV_HEADS
    key_rows = jnp.repeat(key_rows, group_size, axis=1)
    value_rows = jnp.repeat(value_rows, group_size, axis=1)
    block_rows = min(512, LEN)
    positions = jnp.arange(LEN, dtype=jnp.int32)
    score_scale = HEAD_DIM ** (-0.5)

    def attend(row_start):
        query_block = lax.dynamic_slice_in_dim(queries, row_start, block_rows, 0)
        scores = jnp.einsum('qhd,khd->hqk', query_block, key_rows, precision=HIGHEST) * score_scale
        scores = low_back(scores)
        row_index = row_start + jnp.arange(block_rows, dtype=jnp.int32)
        allowed = (positions[None, :] <= row_index[:, None]) & (positions[None, :] < length)
        scores = jnp.where(allowed[None], scores, -1e+30)
        weights = low(jax.nn.softmax(scores, axis=-1))
        return jnp.einsum('hqk,khd->qhd', weights, value_rows, precision=HIGHEST)
    starts = jnp.arange(LEN // block_rows, dtype=jnp.int32) * block_rows
    attended = lax.map(jax.checkpoint(attend), starts).reshape(LEN, HEADS * HEAD_DIM)
    attended = low(low_back(attended))
    hidden_state = tokens + low_back(matmul(attended, out_weight))
    mixed_rows = low(norm_rows(hidden_state, second_gain))
    gate_value = low_back(matmul(mixed_rows, gate_weight))
    up_value = low_back(matmul(mixed_rows, up_weight))
    activated = low(jax.nn.silu(gate_value) * up_value)
    return hidden_state + matmul(activated, down_weight)

def reference(tokens, lengths, cotangent, first_gain, query_weight, key_weight, value_weight, query_gain, key_gain, out_weight, second_gain, gate_weight, up_weight, down_weight):
    parameters = tuple((argument.astype(jnp.float32) for argument in (first_gain, query_weight, key_weight, value_weight, query_gain, key_gain, out_weight, second_gain, gate_weight, up_weight, down_weight)))
    initial = tuple((jnp.zeros(argument.shape, jnp.float32) for argument in parameters))

    def one_sequence(totals, seq_index):
        row_start = (seq_index * LEN).astype(jnp.int32)
        rows_in = lax.dynamic_slice_in_dim(tokens, row_start, LEN, 0).astype(jnp.float32)
        rows_cot = lax.dynamic_slice_in_dim(cotangent, row_start, LEN, 0).astype(jnp.float32)
        length = lengths[seq_index]
        valid_rows = (jnp.arange(LEN, dtype=jnp.int32) < length).astype(jnp.float32)[:, None]
        output, pullback = jax.vjp(partial(forward, length), rows_in, *parameters)
        gradients = pullback(rows_cot * valid_rows)
        totals = tuple((running + update for running, update in zip(totals, gradients[1:])))
        return (totals, (output.astype(jnp.bfloat16), gradients[0].astype(jnp.bfloat16)))
    totals, (outputs, token_grads) = lax.scan(one_sequence, initial, jnp.arange(SEQS, dtype=jnp.int32))
    return (outputs.reshape(TOKENS, D), token_grads.reshape(TOKENS, D), totals[0], totals[1], totals[2], totals[3], totals[4], totals[5], totals[6], totals[7], totals[8], totals[9], totals[10])
```

```python
from functools import partial

import jax
import jax.numpy as jnp
from jax import lax
from jax.sharding import PartitionSpec as P

EPSILON = 1e-06
ROPE_BASE = 1000000.0


def norm_rows(values, gain):
    factor = lax.rsqrt(jnp.mean(values * values, axis=-1, keepdims=True) + EPSILON)
    return values * factor * gain


def rope_tables(seq_len, head_dim):
    half_dim = head_dim // 2
    frequency = ROPE_BASE ** (-(jnp.arange(half_dim, dtype=jnp.float32) * 2.0 / head_dim))
    angles = jnp.arange(seq_len, dtype=jnp.float32)[:, None] * frequency[None, :]
    angles = jnp.concatenate([angles, angles], axis=1)
    return (jnp.cos(angles)[:, None, :], jnp.sin(angles)[:, None, :])


def rotate(values, cosine_table, sine_table):
    half_dim = values.shape[-1] // 2
    turned = jnp.concatenate([-values[..., half_dim:], values[..., :half_dim]], axis=-1)
    return values * cosine_table + turned * sine_table


def head_post(raw_heads, gain, cosine_table, sine_table):
    return rotate(norm_rows(raw_heads, gain), cosine_table, sine_table)


def mask_table(row_start, block_rows, seq_len, length):
    positions = jnp.arange(seq_len, dtype=jnp.int32)
    row_index = row_start + jnp.arange(block_rows, dtype=jnp.int32)
    return (positions[None, :] <= row_index[:, None]) & (positions[None, :] < length)


def small_sum(values, axis, size):
    total = values
    for shift in range(1, size):
        pairs = [(i, (i + shift) % size) for i in range(size)]
        total = total + lax.ppermute(values, axis, pairs)
    return total


def after(value, *others):
    return lax.optimization_barrier((value, others))[0]


def dot(left, right, contract):
    return lax.dot_general(left, right, (contract, ((), ())), preferred_element_type=jnp.float32)


def pair_sum(left, right, core, pairs):
    half = left.shape[1] // 2

    def rows(which):
        part = lax.dynamic_slice_in_dim(left, which * half, half, 1)
        return dot(part, right, ((0,), (0,)))

    received = lax.ppermute(rows(1 - core).astype(jnp.bfloat16), "dp", pairs)
    return (rows(core) + received.astype(jnp.float32)).astype(jnp.bfloat16)


def both_halves(mine, core, pairs):
    other = lax.ppermute(mine, "dp", pairs)
    parts = (jnp.where(core == 0, mine, other), jnp.where(core == 0, other, mine))
    return jnp.concatenate(parts, axis=0).astype(jnp.float32)


def local(
    tensor_size,
    dp_size,
    tokens,
    lengths,
    cotangent,
    first_gain,
    query_weight,
    key_weight,
    value_weight,
    query_gain,
    key_gain,
    out_weight,
    second_gain,
    gate_weight,
    up_weight,
    down_weight,
):
    bf16 = jnp.bfloat16
    tensor_rank = lax.axis_index("tensor")
    dp_rank = lax.axis_index("dp")
    seq_len = tokens.shape[0]
    share_width = tokens.shape[1]
    model_width = first_gain.shape[0]
    head_dim = query_gain.shape[0]
    local_heads = query_weight.shape[1] // head_dim
    local_groups = key_weight.shape[1] // head_dim
    group_size = local_heads // local_groups
    block_rows = min(512, seq_len)
    block_count = seq_len // block_rows
    score_scale = head_dim ** (-0.5)
    length = lengths[0]
    valid_rows = (jnp.arange(seq_len, dtype=jnp.int32) < length).astype(jnp.float32)[:, None]
    own_start = tensor_rank * share_width
    first_own = lax.dynamic_slice_in_dim(first_gain, own_start, share_width, 0)
    second_own = lax.dynamic_slice_in_dim(second_gain, own_start, share_width, 0)
    full_tokens = lax.all_gather(tokens, "tensor", axis=1, tiled=True)
    full_cot = lax.all_gather(after(cotangent, full_tokens), "tensor", axis=1, tiled=True)
    out_cols = model_width // dp_size
    out_rows = out_weight.shape[0]
    out_part = lax.dynamic_slice_in_dim(out_weight, dp_rank * out_cols, out_cols, 1)
    out_full = jnp.zeros((out_rows * tensor_size, model_width), bf16)
    for shift in range(tensor_size):
        pairs = [(i, (i + shift) % tensor_size) for i in range(tensor_size)]
        source = lax.rem(tensor_rank + tensor_size - shift, tensor_size)
        piece = lax.ppermute(out_part, "tensor", pairs) if shift else out_part
        out_full = lax.dynamic_update_slice(
            out_full, piece, (source * out_rows, dp_rank * out_cols)
        )
    rotated_order = [[(i + 1) % dp_size for i in range(dp_size)]]
    out_full = lax.psum(out_full, "dp", axis_index_groups=rotated_order)

    token_own = tokens.astype(jnp.float32)
    token_rows = full_tokens.astype(jnp.float32)
    first_root = lax.rsqrt(jnp.mean(token_rows * token_rows, axis=1, keepdims=True) + EPSILON)
    normed = (token_rows * first_root * first_gain).astype(bf16)
    query_raw = dot(normed, query_weight, ((1,), (0,))).reshape(seq_len, local_heads, head_dim)
    key_raw = dot(normed, key_weight, ((1,), (0,))).reshape(seq_len, local_groups, head_dim)
    value_rows = dot(normed, value_weight, ((1,), (0,))).astype(bf16).reshape(seq_len, local_groups, head_dim)
    cosine_table, sine_table = rope_tables(seq_len, head_dim)
    rotated = partial(head_post, cosine_table=cosine_table, sine_table=sine_table)
    query_rot, query_pull = jax.vjp(rotated, query_raw, query_gain)
    key_rot, key_pull = jax.vjp(rotated, key_raw, key_gain)
    query_rows = query_rot.astype(bf16).reshape(seq_len, local_groups, group_size, head_dim)
    key_rows = key_rot.astype(bf16)

    def block_scores(row_start):
        query_block = lax.dynamic_slice_in_dim(query_rows, row_start, block_rows, 0)
        scores = (
            jnp.einsum("qcgd,kcd->cgqk", query_block, key_rows, preferred_element_type=jnp.float32)
            * score_scale
        )
        allowed = mask_table(row_start, block_rows, seq_len, length)
        return (query_block, jnp.where(allowed[None, None], scores, -1e30))

    def attend(row_start):
        query_block, scores = block_scores(row_start)
        highest = jnp.max(scores, axis=-1, keepdims=True)
        raised = jnp.exp(scores - highest)
        row_total = jnp.sum(raised, axis=-1, keepdims=True)
        weights = (raised / row_total).astype(bf16)
        block_out = jnp.einsum(
            "cgqk,kcd->qcgd", weights, value_rows, preferred_element_type=jnp.float32
        )
        return (block_out, highest + jnp.log(row_total))

    starts = jnp.arange(block_count, dtype=jnp.int32) * block_rows
    attended, log_totals = lax.map(attend, starts)
    attended = attended.reshape(seq_len, local_heads * head_dim).astype(bf16)

    out_full = after(out_full, attended)
    attended = after(attended, full_cot)
    grad_full = (full_cot.astype(jnp.float32) * valid_rows).astype(bf16)
    grad_own = cotangent.astype(jnp.float32) * valid_rows

    half = seq_len // 2
    grad_parts, product_parts, mixed_parts = [], [], []
    gate_grad_parts, up_grad_parts, mid_parts, root_parts, hidden_parts = [], [], [], [], []
    halves = (slice(0, half), slice(half, seq_len))
    heads_in = (attended[:half], after(attended[half:], out_full))
    heads_parts = [lax.all_gather(part, "tensor", axis=1, tiled=True) for part in heads_in]
    product_grads = [dot(grad_full[rows], down_weight, ((1,), (1,))) for rows in halves]
    earlier = product_grads
    for part, rows in enumerate(halves):
        heads_full = after(heads_parts[part], *earlier)
        grad_product = product_grads[part]
        hidden = token_rows[rows] + dot(heads_full, out_full, ((1,), (0,)))
        root = lax.rsqrt(jnp.mean(hidden * hidden, axis=1, keepdims=True) + EPSILON)
        mixed = (hidden * root * second_gain).astype(bf16)
        gate_value = dot(mixed, gate_weight, ((1,), (0,)))
        up_value = dot(mixed, up_weight, ((1,), (0,)))
        sigmoid_gate = jax.nn.sigmoid(gate_value)
        activated = gate_value * sigmoid_gate
        product = (activated * up_value).astype(bf16)
        slope = sigmoid_gate * (1.0 + gate_value * (1.0 - sigmoid_gate))
        gate_grad = (grad_product * up_value * slope).astype(bf16)
        up_grad = (grad_product * activated).astype(bf16)
        mid = jnp.sum(
            gate_grad.astype(jnp.float32) * gate_value + up_grad.astype(jnp.float32) * up_value,
            axis=1,
        )
        mid_parts.append(small_sum(mid, "tensor", tensor_size)[:, None])
        mixed_grad = dot(gate_grad, gate_weight, ((1,), (1,))) + dot(
            up_grad, up_weight, ((1,), (1,))
        )
        mixed_grad = mixed_grad.astype(bf16)
        earlier = [mixed_grad]
        grad_parts.append(lax.psum_scatter(mixed_grad, "tensor", scatter_dimension=1, tiled=True))
        hidden_parts.append(lax.dynamic_slice_in_dim(hidden, own_start, share_width, 1))
        root_parts.append(root)
        product_parts.append(product)
        mixed_parts.append(mixed)
        gate_grad_parts.append(gate_grad)
        up_grad_parts.append(up_grad)
    hidden_own, second_root, product, mixed_rows, gate_grads, up_grads = (
        jnp.concatenate(parts, axis=0)
        for parts in (
            hidden_parts,
            root_parts,
            product_parts,
            mixed_parts,
            gate_grad_parts,
            up_grad_parts,
        )
    )
    down_part = dot(product, down_weight, ((1,), (0,))).astype(bf16)
    core = lax.rem(dp_rank, 2)
    pairs = [(i, i ^ 1) for i in range(dp_size)]
    chips = [[i for i in range(dp_size) if i % 2 == side] for side in (0, 1)]
    early = (
        pair_sum(product, grad_full, core, pairs),
        pair_sum(mixed_rows, gate_grads, core, pairs),
        pair_sum(mixed_rows, up_grads, core, pairs),
    )
    grad_parts, mid_parts = after((grad_parts, mid_parts), *early, down_part)
    mixed_own_grad = jnp.concatenate(grad_parts, axis=0).astype(jnp.float32)
    mid_total = jnp.concatenate(mid_parts, axis=0)
    early = lax.psum(early, "dp", axis_index_groups=chips)

    second_gain_grad = jnp.sum(mixed_own_grad * hidden_own * second_root, axis=0)
    hidden_grad = (
        grad_own
        + mixed_own_grad * second_own * second_root
        - hidden_own * second_root**2 / model_width * mid_total
    )
    hidden_grad_rows = lax.all_gather(hidden_grad.astype(bf16), "tensor", axis=1, tiled=True)
    down_part, hidden_grad_rows = lax.optimization_barrier((down_part, hidden_grad_rows))
    down_own = lax.psum_scatter(down_part, "tensor", scatter_dimension=1, tiled=True)
    grad_out = pair_sum(attended, hidden_grad_rows, core, pairs)
    attended_grad = (
        dot(hidden_grad_rows, out_weight, ((1,), (1,)))
        .astype(bf16)
        .reshape(seq_len, local_groups, group_size, head_dim)
    )

    def attend_back(running, row_start):
        key_sum, value_sum = running
        query_block, scores = block_scores(row_start)
        block_index = row_start // block_rows
        weights = jnp.exp(scores - log_totals[block_index])
        grad_block = lax.dynamic_slice_in_dim(attended_grad, row_start, block_rows, 0)
        weight_grad = jnp.einsum(
            "qcgd,kcd->cgqk", grad_block, value_rows, preferred_element_type=jnp.float32
        )
        centre = jnp.sum(weights * weight_grad, axis=-1, keepdims=True)
        score_grad = (weights * (weight_grad - centre)).astype(bf16)
        value_sum = value_sum + jnp.einsum(
            "cgqk,qcgd->kcd",
            weights.astype(bf16),
            grad_block,
            preferred_element_type=jnp.float32,
        )
        key_sum = (
            key_sum
            + jnp.einsum(
                "cgqk,qcgd->kcd", score_grad, query_block, preferred_element_type=jnp.float32
            )
            * score_scale
        )
        query_grad = (
            jnp.einsum("cgqk,kcd->qcgd", score_grad, key_rows, preferred_element_type=jnp.float32)
            * score_scale
        )
        return ((key_sum, value_sum), query_grad)

    empty_groups = jnp.zeros((seq_len, local_groups, head_dim), jnp.float32)
    (key_grad_rot, value_grad), query_blocks = lax.scan(
        attend_back, (empty_groups, empty_groups), starts
    )
    query_grad_rot = query_blocks.reshape(seq_len, local_heads, head_dim)
    query_raw_grad, query_gain_grad = query_pull(query_grad_rot)
    key_raw_grad, key_gain_grad = key_pull(key_grad_rot)
    query_raw_grad = query_raw_grad.reshape(seq_len, local_heads * head_dim).astype(bf16)
    key_raw_grad = key_raw_grad.reshape(seq_len, local_groups * head_dim).astype(bf16)
    value_raw_grad = value_grad.reshape(seq_len, local_groups * head_dim).astype(bf16)
    normed_grad = (
        dot(query_raw_grad, query_weight, ((1,), (1,)))
        + dot(key_raw_grad, key_weight, ((1,), (1,)))
        + dot(value_raw_grad, value_weight, ((1,), (1,)))
    )
    normed_grad = normed_grad.astype(bf16)
    normed_own_grad = lax.psum_scatter(normed_grad, "tensor", scatter_dimension=1, tiled=True)
    late = (
        grad_out,
        pair_sum(normed, query_raw_grad, core, pairs),
        pair_sum(normed, key_raw_grad, core, pairs),
        pair_sum(normed, value_raw_grad, core, pairs),
    )
    down_own = after(down_own, normed_grad, *late)
    layer_out = (hidden_own + down_own.astype(jnp.float32)).astype(bf16)
    normed_own_grad = after(normed_own_grad, layer_out, *early).astype(jnp.float32)
    backwards = [group[::-1] for group in chips]
    late = lax.psum(after(late, normed_grad, *early), "dp", axis_index_groups=backwards)
    grad_down, grad_gate, grad_up = (both_halves(part, core, pairs) for part in early)
    grad_out, grad_query, grad_key, grad_value = (both_halves(part, core, pairs) for part in late)
    first_term, query_gain_grad, key_gain_grad = lax.psum(
        (
            jnp.sum(normed_own_grad * first_own * token_own, axis=1, keepdims=True),
            query_gain_grad,
            key_gain_grad,
        ),
        "tensor",
    )
    first_gain_grad = jnp.sum(normed_own_grad * token_own * first_root, axis=0)
    token_grad = (
        hidden_grad
        + normed_own_grad * first_own * first_root
        - token_own * first_root**3 / model_width * first_term
    ).astype(bf16)
    gains = jnp.concatenate([first_gain_grad, second_gain_grad, query_gain_grad, key_gain_grad])
    gains = lax.psum(gains, "dp")
    first_gain_grad, second_gain_grad, query_gain_grad, key_gain_grad = (
        gains[:share_width],
        gains[share_width : 2 * share_width],
        gains[2 * share_width : 2 * share_width + head_dim],
        gains[2 * share_width + head_dim :],
    )
    return (
        layer_out,
        token_grad,
        first_gain_grad,
        grad_query,
        grad_key,
        grad_value,
        query_gain_grad,
        key_gain_grad,
        grad_out,
        second_gain_grad,
        grad_gate,
        grad_up,
        grad_down,
    )


def solution(mesh):
    in_specs = (
        P("dp", "tensor"),
        P("dp"),
        P("dp", "tensor"),
        P(),
        P(None, "tensor"),
        P(None, "tensor"),
        P(None, "tensor"),
        P(),
        P(),
        P("tensor", None),
        P(),
        P(None, "tensor"),
        P(None, "tensor"),
        P("tensor", None),
    )
    out_specs = (
        P("dp", "tensor"),
        P("dp", "tensor"),
        P("tensor"),
        P(None, "tensor"),
        P(None, "tensor"),
        P(None, "tensor"),
        P(),
        P(),
        P("tensor", None),
        P("tensor"),
        P(None, "tensor"),
        P(None, "tensor"),
        P("tensor", None),
    )
    return jax.shard_map(
        partial(local, mesh.shape["tensor"], mesh.shape["dp"]), mesh=mesh, in_specs=in_specs, out_specs=out_specs, check_vma=False)
```

```python
import math
from functools import partial

import jax
import jax.numpy as jnp
from jax import lax
from jax.experimental import pallas as pl
from jax.experimental.pallas import tpu as pltpu
from jax.sharding import PartitionSpec as P

EPSILON = 1e-06
ROPE_BASE = 1000000.0


def rope_tables(seq_len, head_dim):
    half_dim = head_dim // 2
    frequency = ROPE_BASE ** (-(jnp.arange(half_dim, dtype=jnp.float32) * 2.0 / head_dim))
    angles = jnp.arange(seq_len, dtype=jnp.float32)[:, None] * frequency[None, :]
    angles = jnp.concatenate([angles, angles], axis=1)
    return (jnp.cos(angles)[:, None, :], jnp.sin(angles)[:, None, :])


def rope_rows(seq_len, head_dim):
    cosine, sine = rope_tables(seq_len, head_dim)
    signs = jnp.where(jnp.arange(head_dim) < head_dim // 2, -1.0, 1.0)
    return cosine[:, 0, :], sine[:, 0, :] * signs[None, :]


def head_factor(raw):
    return lax.rsqrt(jnp.mean(raw * raw, axis=-1, keepdims=True) + EPSILON)


def turn(values):
    return pltpu.roll(values, values.shape[-1] // 2, 1)


def dot(left, right, contract):
    return lax.dot_general(left, right, (contract, ((), ())), preferred_element_type=jnp.float32)


def attention_kernel(
    group_size,
    block,
    length_ref,
    query_ref,
    key_ref,
    value_ref,
    query_gain_ref,
    key_gain_ref,
    cosine_ref,
    sine_ref,
    out_ref,
    query_out_ref,
    key_out_ref,
):
    seq_len, head_dim = query_ref.shape
    scale = head_dim ** (-0.5)
    length = length_ref[0]

    def post(raw, gain):
        normed = raw * head_factor(raw) * gain
        return (normed * cosine_ref[...] + turn(normed) * sine_ref[...]).astype(jnp.bfloat16)

    @pl.when(lax.rem(pl.program_id(0), group_size) == 0)
    def _():
        key_out_ref[...] = post(key_ref[...], key_gain_ref[...])

    query_out_ref[...] = post(query_ref[...], query_gain_ref[...])
    below = lax.broadcasted_iota(jnp.int32, (block, block), 0) >= lax.broadcasted_iota(
        jnp.int32, (block, block), 1
    )
    for start in range(0, seq_len, block):
        queries = query_out_ref[start : start + block, :]
        parts = []
        for first, count in ((0, start), (start, block)):
            if not count:
                continue
            scores = dot(queries, key_out_ref[first : first + count, :], ((1,), (1,))) * scale
            place = first + lax.broadcasted_iota(jnp.int32, (1, count), 1)
            scores = scores + jnp.where(place < length, 0.0, -1e30)
            if first == start:
                scores = jnp.where(below, scores, -1e30)
            parts.append((first, count, scores))
        highest = parts[0][2].max(axis=1, keepdims=True)
        for _, _, scores in parts[1:]:
            highest = jnp.maximum(highest, scores.max(axis=1, keepdims=True))
        total, result = 0.0, 0.0
        for first, count, scores in parts:
            raised = jnp.exp(scores - highest)
            total = total + raised.sum(axis=1, keepdims=True)
            values = value_ref[first : first + count, :]
            result = result + dot(raised.astype(jnp.bfloat16), values, ((1,), (0,)))
        out_ref[start : start + block, :] = (result / total).astype(jnp.bfloat16)


def attention_back_kernel(
    group_size,
    block,
    length_ref,
    query_ref,
    key_ref,
    value_ref,
    query_raw_ref,
    key_raw_ref,
    grad_ref,
    query_gain_ref,
    key_gain_ref,
    cosine_ref,
    sine_ref,
    query_grad_ref,
    key_grad_ref,
    value_grad_ref,
    query_gain_grad_ref,
    key_gain_grad_ref,
    query_sum,
    key_sum,
    value_sum,
):
    seq_len, head_dim = query_ref.shape
    scale = head_dim ** (-0.5)
    length = length_ref[0]
    head = pl.program_id(0)
    place_in_group = lax.rem(head, group_size)

    @pl.when(head == 0)
    def _():
        query_gain_grad_ref[...] = jnp.zeros_like(query_gain_grad_ref)
        key_gain_grad_ref[...] = jnp.zeros_like(key_gain_grad_ref)

    @pl.when(place_in_group == 0)
    def _():
        key_sum[...] = jnp.zeros_like(key_sum)
        value_sum[...] = jnp.zeros_like(value_sum)

    above = lax.broadcasted_iota(jnp.int32, (block, block), 0) <= lax.broadcasted_iota(
        jnp.int32, (block, block), 1
    )
    for start in range(0, seq_len, block):
        rows = slice(start, start + block)
        queries, grads = query_ref[rows, :], grad_ref[rows, :]
        parts = []
        for first, count in ((0, start), (start, block)):
            if not count:
                continue
            scores = dot(key_ref[first : first + count, :], queries, ((1,), (1,))) * scale
            place = first + lax.broadcasted_iota(jnp.int32, (count, 1), 0)
            scores = jnp.where(place < length, scores, -1e30)
            if first == start:
                scores = jnp.where(above, scores, -1e30)
            parts.append((slice(first, first + count), scores))
        highest = parts[0][1].max(axis=0, keepdims=True)
        for _, scores in parts[1:]:
            highest = jnp.maximum(highest, scores.max(axis=0, keepdims=True))
        parts = [(keys, jnp.exp(scores - highest)) for keys, scores in parts]
        total = sum(raised.sum(axis=0, keepdims=True) for _, raised in parts)
        inverse = 1.0 / total
        centre, weighted = 0.0, []
        for keys, raised in parts:
            weights = raised * inverse
            weight_grad = dot(value_ref[keys, :], grads, ((1,), (1,)))
            centre = centre + (weights * weight_grad).sum(axis=0, keepdims=True)
            value_sum[keys, :] += dot(weights.astype(jnp.bfloat16), grads, ((1,), (0,)))
            weighted.append((keys, weights, weight_grad))
        query_grad = 0.0
        for keys, weights, weight_grad in weighted:
            score_grad = (weights * (weight_grad - centre)).astype(jnp.bfloat16)
            key_sum[keys, :] += dot(score_grad, queries, ((1,), (0,)))
            query_grad = query_grad + dot(score_grad, key_ref[keys, :], ((0,), (0,)))
        query_sum[rows, :] = query_grad

    def back(total, raw, gain):
        grad = total * scale
        grad = grad * cosine_ref[...] - turn(grad) * sine_ref[...]
        factor = head_factor(raw)
        gain_grad = (grad * raw * factor).sum(axis=0, keepdims=True)
        grad = grad * gain
        shift = (grad * raw).sum(axis=1, keepdims=True) * (factor * factor * factor / head_dim)
        return (grad * factor - raw * shift).astype(jnp.bfloat16), gain_grad

    query_grad_ref[...], gain_grad = back(query_sum[...], query_raw_ref[...], query_gain_ref[...])
    query_gain_grad_ref[...] += gain_grad

    @pl.when(place_in_group == group_size - 1)
    def _():
        key_grad_ref[...], gain_grad = back(key_sum[...], key_raw_ref[...], key_gain_ref[...])
        key_gain_grad_ref[...] += gain_grad
        value_grad_ref[...] = value_sum[...].astype(jnp.bfloat16)


def attention_specs(seq_len, head_dim, group_size):
    query = pl.BlockSpec((seq_len, head_dim), lambda head: (0, head))
    key = pl.BlockSpec((seq_len, head_dim), lambda head: (0, head // group_size))
    gain = pl.BlockSpec((1, head_dim), lambda head: (0, 0))
    table = pl.BlockSpec((seq_len, head_dim), lambda head: (0, 0))
    length = pl.BlockSpec(memory_space=pltpu.SMEM)
    return length, query, key, gain, table


def attention(length, query_raw, key_raw, values, query_gain, key_gain, cosine, sine, group_size):
    seq_len, head_dim = cosine.shape
    heads = query_raw.shape[1] // head_dim
    block = math.gcd(256, seq_len)
    count, query, key, gain, table = attention_specs(seq_len, head_dim, group_size)
    pairs = heads * seq_len * (seq_len + block) // 2
    return pl.pallas_call(
        partial(attention_kernel, group_size, block),
        grid=(heads,),
        in_specs=[count, query, key, key, gain, gain, table, table],
        out_specs=[query, query, key],
        out_shape=[
            jax.ShapeDtypeStruct(query_raw.shape, jnp.bfloat16),
            jax.ShapeDtypeStruct(query_raw.shape, jnp.bfloat16),
            jax.ShapeDtypeStruct(key_raw.shape, jnp.bfloat16),
        ],
        compiler_params=pltpu.CompilerParams(vmem_limit_bytes=40 * 1024 * 1024),
        cost_estimate=pl.CostEstimate(
            flops=4 * pairs * head_dim, bytes_accessed=8 * query_raw.size, transcendentals=pairs
        ),
        name="attention",
    )(length, query_raw, key_raw, values, query_gain, key_gain, cosine, sine)


def attention_back(
    length,
    queries,
    keys,
    values,
    query_raw,
    key_raw,
    grads,
    query_gain,
    key_gain,
    cosine,
    sine,
    group_size,
):
    seq_len, head_dim = cosine.shape
    heads = query_raw.shape[1] // head_dim
    block = math.gcd(256, seq_len)
    count, query, key, gain, table = attention_specs(seq_len, head_dim, group_size)
    pairs = heads * seq_len * (seq_len + block) // 2
    rows = pltpu.VMEM((seq_len, head_dim), jnp.float32)
    return pl.pallas_call(
        partial(attention_back_kernel, group_size, block),
        grid=(heads,),
        in_specs=[count, query, key, key, query, key, query, gain, gain, table, table],
        out_specs=[query, key, key, gain, gain],
        out_shape=[
            jax.ShapeDtypeStruct(queries.shape, jnp.bfloat16),
            jax.ShapeDtypeStruct(keys.shape, jnp.bfloat16),
            jax.ShapeDtypeStruct(keys.shape, jnp.bfloat16),
            jax.ShapeDtypeStruct((1, head_dim), jnp.float32),
            jax.ShapeDtypeStruct((1, head_dim), jnp.float32),
        ],
        scratch_shapes=[rows, rows, rows],
        compiler_params=pltpu.CompilerParams(vmem_limit_bytes=40 * 1024 * 1024),
        cost_estimate=pl.CostEstimate(
            flops=10 * pairs * head_dim, bytes_accessed=12 * query_raw.size, transcendentals=pairs
        ),
        name="attention_back",
    )(length, queries, keys, values, query_raw, key_raw, grads, query_gain, key_gain, cosine, sine)


def feed_kernel(branch_steps, own_width, first_half, *refs):
    rank_ref, heads_ref, token_ref, grad_ref, out_ref, gain_ref = refs[:6]
    gate_ref, up_ref, down_ref = refs[6:9]
    refs = refs[9:] if first_half else refs[15:]
    mixed_ref, product_ref, gate_grad_ref, up_grad_ref, own_ref, root_ref = refs[:6]
    mid_ref, mixed_grad_ref, hidden, total, squares, mid = refs[6:]
    step = pl.program_id(0)
    width = out_ref.shape[1]

    @pl.when(step == 0)
    def _():
        squares[...] = jnp.zeros_like(squares)

    @pl.when(step < branch_steps)
    def _():
        part = token_ref[...].astype(jnp.float32) + dot(heads_ref[...], out_ref[...], ((1,), (0,)))
        hidden[:, pl.ds(pl.multiple_of(step * width, width), width)] = part
        squares[...] += (part * part).sum(axis=1, keepdims=True)

    @pl.when(step == branch_steps)
    def _():
        root = lax.rsqrt(squares[...] / hidden.shape[1] + EPSILON)
        root_ref[...] = root
        mixed_ref[...] = (hidden[...] * root * gain_ref[...]).astype(jnp.bfloat16)
        own_start = pl.multiple_of(rank_ref[0] * own_width, own_width)
        own_ref[...] = hidden[:, pl.ds(own_start, own_width)]
        total[...] = jnp.zeros_like(total)
        mid[...] = jnp.zeros_like(mid)

    @pl.when(step >= branch_steps)
    def _():
        gate = dot(mixed_ref[...], gate_ref[...], ((1,), (0,)))
        up = dot(mixed_ref[...], up_ref[...], ((1,), (0,)))
        product_grad = dot(grad_ref[...], down_ref[...], ((1,), (1,)))
        sigmoid = jax.nn.sigmoid(gate)
        activated = gate * sigmoid
        product_ref[...] = (activated * up).astype(jnp.bfloat16)
        slope = sigmoid * (1.0 + gate * (1.0 - sigmoid))
        gate_grad = (product_grad * up * slope).astype(jnp.bfloat16)
        up_grad = (product_grad * activated).astype(jnp.bfloat16)
        gate_grad_ref[...] = gate_grad
        up_grad_ref[...] = up_grad
        terms = gate_grad.astype(jnp.float32) * gate + up_grad.astype(jnp.float32) * up
        mid[...] += terms.sum(axis=1, keepdims=True)
        total[...] += dot(gate_grad, gate_ref[...], ((1,), (1,)))
        total[...] += dot(up_grad, up_ref[...], ((1,), (1,)))

    @pl.when(step == pl.num_programs(0) - 1)
    def _():
        mixed_grad_ref[...] = total[...].astype(jnp.bfloat16)
        mid_ref[...] = mid[...]


def feed_forward(part, earlier, rank, heads, tokens, grads, out_full, gain, gate, up, down, own):
    seq_len, model_width = tokens.shape
    half, hidden_width = seq_len // 2, gate.shape[1]
    wide = math.gcd(512, model_width)
    tile = math.gcd(512, hidden_width)
    branch_steps = model_width // wide
    steps = branch_steps + hidden_width // tile

    def first(step):
        return jnp.minimum(step, branch_steps - 1)

    def second(step):
        return jnp.maximum(step - branch_steps, 0)

    once = pl.Buffered(1)
    f32, bf16 = jnp.float32, jnp.bfloat16
    in_specs = [
        pl.BlockSpec(memory_space=pltpu.SMEM),
        pl.BlockSpec((half, heads.shape[1]), lambda i: (0, 0), pipeline_mode=once),
        pl.BlockSpec((half, wide), lambda i: (part, first(i))),
        pl.BlockSpec((half, model_width), lambda i: (part, 0), pipeline_mode=once),
        pl.BlockSpec((out_full.shape[0], wide), lambda i: (0, first(i))),
        pl.BlockSpec((1, model_width), lambda i: (0, 0)),
        pl.BlockSpec((model_width, tile), lambda i: (0, second(i))),
        pl.BlockSpec((model_width, tile), lambda i: (0, second(i))),
        pl.BlockSpec((tile, model_width), lambda i: (second(i), 0)),
    ]
    in_specs += [pl.BlockSpec(memory_space=pl.ANY)] * len(earlier)
    inner = pl.BlockSpec((half, tile), lambda i: (part, second(i)))
    out_specs = [
        pl.BlockSpec((half, model_width), lambda i: (part, 0), pipeline_mode=once),
        inner,
        inner,
        inner,
        pl.BlockSpec((half, own), lambda i: (part, 0), pipeline_mode=once),
        pl.BlockSpec((half, 1), lambda i: (part, 0), pipeline_mode=once),
        pl.BlockSpec((half, 1), lambda i: (0, 0), pipeline_mode=once),
        pl.BlockSpec((half, model_width), lambda i: (0, 0), pipeline_mode=once),
    ]
    out_shape = [
        jax.ShapeDtypeStruct((seq_len, model_width), bf16),
        jax.ShapeDtypeStruct((seq_len, hidden_width), bf16),
        jax.ShapeDtypeStruct((seq_len, hidden_width), bf16),
        jax.ShapeDtypeStruct((seq_len, hidden_width), bf16),
        jax.ShapeDtypeStruct((seq_len, own), f32),
        jax.ShapeDtypeStruct((seq_len, 1), f32),
        jax.ShapeDtypeStruct((half, 1), f32),
        jax.ShapeDtypeStruct((half, model_width), bf16),
    ]
    return pl.pallas_call(
        partial(feed_kernel, branch_steps, own, not earlier),
        grid=(steps,),
        in_specs=in_specs,
        out_specs=out_specs,
        out_shape=out_shape,
        input_output_aliases={9 + i: i for i in range(len(earlier))},
        scratch_shapes=[
            pltpu.VMEM((half, model_width), f32),
            pltpu.VMEM((half, model_width), f32),
            pltpu.VMEM((half, 1), f32),
            pltpu.VMEM((half, 1), f32),
        ],
        compiler_params=pltpu.CompilerParams(vmem_limit_bytes=58 * 1024 * 1024),
        cost_estimate=pl.CostEstimate(
            flops=2 * half * model_width * (heads.shape[1] + 5 * hidden_width),
            bytes_accessed=2 * (out_full.size + gate.size + up.size + down.size),
            transcendentals=half * hidden_width,
        ),
        name="feed_forward",
    )(rank, heads, tokens, grads, out_full, gain, gate, up, down, *earlier)


def small_sum(values, axis, size):
    total = values
    for shift in range(1, size):
        pairs = [(i, (i + shift) % size) for i in range(size)]
        total = total + lax.ppermute(values, axis, pairs)
    return total


def after(value, *others):
    return lax.optimization_barrier((value, others))[0]


def pair_sum(left, right, core, pairs):
    half = left.shape[1] // 2

    def rows(which):
        part = lax.dynamic_slice_in_dim(left, which * half, half, 1)
        return dot(part, right, ((0,), (0,)))

    received = lax.ppermute(rows(1 - core).astype(jnp.bfloat16), "dp", pairs)
    return (rows(core) + received.astype(jnp.float32)).astype(jnp.bfloat16)


def both_halves(mine, core, pairs):
    other = lax.ppermute(mine, "dp", pairs)
    parts = (jnp.where(core == 0, mine, other), jnp.where(core == 0, other, mine))
    return jnp.concatenate(parts, axis=0).astype(jnp.float32)


def local(
    tensor_size,
    dp_size,
    tokens,
    lengths,
    cotangent,
    first_gain,
    query_weight,
    key_weight,
    value_weight,
    query_gain,
    key_gain,
    out_weight,
    second_gain,
    gate_weight,
    up_weight,
    down_weight,
):
    bf16 = jnp.bfloat16
    tensor_rank = lax.axis_index("tensor")
    dp_rank = lax.axis_index("dp")
    seq_len = tokens.shape[0]
    share_width = tokens.shape[1]
    model_width = first_gain.shape[0]
    head_dim = query_gain.shape[0]
    local_heads = query_weight.shape[1] // head_dim
    local_groups = key_weight.shape[1] // head_dim
    group_size = local_heads // local_groups
    length = lengths[0]
    valid_rows = (jnp.arange(seq_len, dtype=jnp.int32) < length).astype(jnp.float32)[:, None]
    own_start = tensor_rank * share_width
    first_own = lax.dynamic_slice_in_dim(first_gain, own_start, share_width, 0)
    second_own = lax.dynamic_slice_in_dim(second_gain, own_start, share_width, 0)
    full_tokens = lax.all_gather(tokens, "tensor", axis=1, tiled=True)
    out_cols = model_width // dp_size
    out_rows = out_weight.shape[0]
    out_part = lax.dynamic_slice_in_dim(out_weight, dp_rank * out_cols, out_cols, 1)
    pieces = [out_part]
    for shift in range(1, tensor_size):
        ring = [(i, (i + shift) % tensor_size) for i in range(tensor_size)]
        pieces.append(lax.ppermute(out_part, "tensor", ring))
    full_tokens = after(full_tokens, *pieces)
    full_cot = lax.all_gather(after(cotangent, full_tokens), "tensor", axis=1, tiled=True)
    out_block = jnp.zeros((out_rows * tensor_size, out_cols), bf16)
    for shift, piece in enumerate(pieces):
        source = lax.rem(tensor_rank + tensor_size - shift, tensor_size)
        out_block = lax.dynamic_update_slice_in_dim(out_block, piece, source * out_rows, 0)
    out_full = jnp.zeros((out_rows * tensor_size, model_width), bf16)
    out_full = lax.dynamic_update_slice_in_dim(out_full, out_block, dp_rank * out_cols, 1)
    rotated_order = [[(i + 1) % dp_size for i in range(dp_size)]]
    out_full = lax.psum(out_full, "dp", axis_index_groups=rotated_order)

    token_own = tokens.astype(jnp.float32)
    token_rows = full_tokens.astype(jnp.float32)
    first_root = lax.rsqrt(jnp.mean(token_rows * token_rows, axis=1, keepdims=True) + EPSILON)
    normed = (token_rows * first_root * first_gain).astype(bf16)
    query_raw = dot(normed, query_weight, ((1,), (0,)))
    key_raw = dot(normed, key_weight, ((1,), (0,)))
    value_rows = dot(normed, value_weight, ((1,), (0,))).astype(bf16)
    cosine, sine = rope_rows(seq_len, head_dim)
    head_gains = (query_gain[None, :], key_gain[None, :])
    attended, query_rows, key_rows = attention(
        lengths, query_raw, key_raw, value_rows, *head_gains, cosine, sine, group_size
    )

    out_full = after(out_full, attended)
    attended = after(attended, full_cot)
    grad_full = (full_cot.astype(jnp.float32) * valid_rows).astype(bf16)
    grad_own = cotangent.astype(jnp.float32) * valid_rows

    half = seq_len // 2
    heads_in = (attended[:half], after(attended[half:], out_full))
    heads_parts = [lax.all_gather(part, "tensor", axis=1, tiled=True) for part in heads_in]
    rank = tensor_rank.astype(jnp.int32)[None]
    grad_parts, mid_parts, kept = [], [], []
    for part, heads_full in enumerate(heads_parts):
        *kept, mid, mixed_grad = feed_forward(
            part,
            kept,
            rank,
            heads_full,
            full_tokens,
            grad_full,
            out_full,
            second_gain[None, :],
            gate_weight,
            up_weight,
            down_weight,
            share_width,
        )
        mid_parts.append(small_sum(mid[:, 0], "tensor", tensor_size)[:, None])
        grad_parts.append(lax.psum_scatter(mixed_grad, "tensor", scatter_dimension=1, tiled=True))
    mixed_rows, product, gate_grads, up_grads, hidden_own, second_root = kept
    core = lax.rem(dp_rank, 2)
    pairs = [(i, i ^ 1) for i in range(dp_size)]
    chips = [[i for i in range(dp_size) if i % 2 == side] for side in (0, 1)]
    early = (
        pair_sum(product, grad_full, core, pairs),
        pair_sum(mixed_rows, gate_grads, core, pairs),
        pair_sum(mixed_rows, up_grads, core, pairs),
    )
    down_part = dot(after(product, *early), down_weight, ((1,), (0,))).astype(bf16)
    grad_parts, mid_parts = after((grad_parts, mid_parts), *early)
    mixed_own_grad = jnp.concatenate(grad_parts, axis=0).astype(jnp.float32)
    mid_total = jnp.concatenate(mid_parts, axis=0)
    early = lax.psum(early, "dp", axis_index_groups=chips)

    second_gain_grad = jnp.sum(mixed_own_grad * hidden_own * second_root, axis=0)
    hidden_grad = (
        grad_own
        + mixed_own_grad * second_own * second_root
        - hidden_own * second_root**2 / model_width * mid_total
    )
    hidden_grad_rows = lax.all_gather(hidden_grad.astype(bf16), "tensor", axis=1, tiled=True)
    down_part, hidden_grad_rows = lax.optimization_barrier((down_part, hidden_grad_rows))
    down_own = lax.psum_scatter(down_part, "tensor", scatter_dimension=1, tiled=True)
    grad_out = pair_sum(attended, hidden_grad_rows, core, pairs)
    attended_grad = dot(hidden_grad_rows, out_weight, ((1,), (1,))).astype(bf16)
    query_raw_grad, key_raw_grad, value_raw_grad, query_gain_grad, key_gain_grad = attention_back(
        lengths,
        query_rows,
        key_rows,
        value_rows,
        query_raw,
        key_raw,
        attended_grad,
        *head_gains,
        cosine,
        sine,
        group_size,
    )
    query_gain_grad, key_gain_grad = query_gain_grad[0], key_gain_grad[0]
    normed_grad = (
        dot(query_raw_grad, query_weight, ((1,), (1,)))
        + dot(key_raw_grad, key_weight, ((1,), (1,)))
        + dot(value_raw_grad, value_weight, ((1,), (1,)))
    )
    normed_grad = normed_grad.astype(bf16)
    normed_own_grad = lax.psum_scatter(normed_grad, "tensor", scatter_dimension=1, tiled=True)
    late = (
        grad_out,
        pair_sum(normed, query_raw_grad, core, pairs),
        pair_sum(normed, key_raw_grad, core, pairs),
        pair_sum(normed, value_raw_grad, core, pairs),
    )
    early = after(early, *late)
    down_own = after(down_own, normed_grad, *late)
    layer_out = (hidden_own + down_own.astype(jnp.float32)).astype(bf16)
    normed_own_grad = after(normed_own_grad, layer_out, *early).astype(jnp.float32)
    backwards = [group[::-1] for group in chips]
    late = lax.psum(after(late, normed_grad, *early), "dp", axis_index_groups=backwards)
    grad_down, grad_gate, grad_up = (both_halves(part, core, pairs) for part in early)
    grad_out, grad_query, grad_key, grad_value = (both_halves(part, core, pairs) for part in late)
    first_term, query_gain_grad, key_gain_grad = lax.psum(
        (
            jnp.sum(normed_own_grad * first_own * token_own, axis=1, keepdims=True),
            query_gain_grad,
            key_gain_grad,
        ),
        "tensor",
    )
    first_gain_grad = jnp.sum(normed_own_grad * token_own * first_root, axis=0)
    token_grad = (
        hidden_grad
        + normed_own_grad * first_own * first_root
        - token_own * first_root**3 / model_width * first_term
    ).astype(bf16)
    gains = jnp.concatenate([first_gain_grad, second_gain_grad, query_gain_grad, key_gain_grad])
    gains = lax.psum(gains, "dp")
    first_gain_grad, second_gain_grad, query_gain_grad, key_gain_grad = (
        gains[:share_width],
        gains[share_width : 2 * share_width],
        gains[2 * share_width : 2 * share_width + head_dim],
        gains[2 * share_width + head_dim :],
    )
    return (
        layer_out,
        token_grad,
        first_gain_grad,
        grad_query,
        grad_key,
        grad_value,
        query_gain_grad,
        key_gain_grad,
        grad_out,
        second_gain_grad,
        grad_gate,
        grad_up,
        grad_down,
    )


def solution(mesh):
    in_specs = (
        P("dp", "tensor"),
        P("dp"),
        P("dp", "tensor"),
        P(),
        P(None, "tensor"),
        P(None, "tensor"),
        P(None, "tensor"),
        P(),
        P(),
        P("tensor", None),
        P(),
        P(None, "tensor"),
        P(None, "tensor"),
        P("tensor", None),
    )
    out_specs = (
        P("dp", "tensor"),
        P("dp", "tensor"),
        P("tensor"),
        P(None, "tensor"),
        P(None, "tensor"),
        P(None, "tensor"),
        P(),
        P(),
        P("tensor", None),
        P("tensor"),
        P(None, "tensor"),
        P(None, "tensor"),
        P("tensor", None),
    )
    return jax.shard_map(
        partial(local, mesh.shape["tensor"], mesh.shape["dp"]), mesh=mesh, in_specs=in_specs, out_specs=out_specs, check_vma=False)
```

```python
import math
from functools import partial

import jax
import jax.numpy as jnp
from jax import lax
from jax.experimental import pallas as pl
from jax.experimental.pallas import tpu as pltpu
from jax.sharding import PartitionSpec as P

EPSILON = 1e-06
ROPE_BASE = 1000000.0


def rope_tables(seq_len, head_dim):
    half_dim = head_dim // 2
    frequency = ROPE_BASE ** (-(jnp.arange(half_dim, dtype=jnp.float32) * 2.0 / head_dim))
    angles = jnp.arange(seq_len, dtype=jnp.float32)[:, None] * frequency[None, :]
    angles = jnp.concatenate([angles, angles], axis=1)
    return (jnp.cos(angles)[:, None, :], jnp.sin(angles)[:, None, :])


def rope_rows(seq_len, head_dim):
    cosine, sine = rope_tables(seq_len, head_dim)
    signs = jnp.where(jnp.arange(head_dim) < head_dim // 2, -1.0, 1.0)
    return cosine[:, 0, :], sine[:, 0, :] * signs[None, :]


def head_factor(raw):
    return lax.rsqrt(jnp.mean(raw * raw, axis=-1, keepdims=True) + EPSILON)


def turn(values):
    return pltpu.roll(values, values.shape[-1] // 2, 1)


def dot(left, right, contract):
    return lax.dot_general(left, right, (contract, ((), ())), preferred_element_type=jnp.float32)


def attention_kernel(
    group_size,
    block,
    length_ref,
    query_ref,
    key_ref,
    value_ref,
    query_gain_ref,
    key_gain_ref,
    cosine_ref,
    sine_ref,
    out_ref,
    query_out_ref,
    key_out_ref,
):
    seq_len, head_dim = query_ref.shape
    scale = head_dim ** (-0.5)
    length = length_ref[0]

    def post(raw, gain):
        normed = raw * head_factor(raw) * gain
        return (normed * cosine_ref[...] + turn(normed) * sine_ref[...]).astype(jnp.bfloat16)

    @pl.when(lax.rem(pl.program_id(0), group_size) == 0)
    def _():
        key_out_ref[...] = post(key_ref[...], key_gain_ref[...])

    query_out_ref[...] = post(query_ref[...], query_gain_ref[...])
    below = lax.broadcasted_iota(jnp.int32, (block, block), 0) >= lax.broadcasted_iota(
        jnp.int32, (block, block), 1
    )
    for start in range(0, seq_len, block):
        queries = query_out_ref[start : start + block, :]
        parts = []
        for first, count in ((0, start), (start, block)):
            if not count:
                continue
            scores = dot(queries, key_out_ref[first : first + count, :], ((1,), (1,))) * scale
            place = first + lax.broadcasted_iota(jnp.int32, (1, count), 1)
            scores = scores + jnp.where(place < length, 0.0, -1e30)
            if first == start:
                scores = jnp.where(below, scores, -1e30)
            parts.append((first, count, scores))
        highest = parts[0][2].max(axis=1, keepdims=True)
        for _, _, scores in parts[1:]:
            highest = jnp.maximum(highest, scores.max(axis=1, keepdims=True))
        total, result = 0.0, 0.0
        for first, count, scores in parts:
            raised = jnp.exp(scores - highest)
            total = total + raised.sum(axis=1, keepdims=True)
            values = value_ref[first : first + count, :].astype(jnp.bfloat16)
            result = result + dot(raised.astype(jnp.bfloat16), values, ((1,), (0,)))
        out_ref[start : start + block, :] = (result / total).astype(jnp.bfloat16)


def attention_back_kernel(
    group_size,
    block,
    length_ref,
    query_ref,
    key_ref,
    query_raw_ref,
    key_raw_ref,
    value_raw_ref,
    grad_ref,
    query_gain_ref,
    key_gain_ref,
    cosine_ref,
    sine_ref,
    query_grad_ref,
    key_grad_ref,
    value_grad_ref,
    query_gain_grad_ref,
    key_gain_grad_ref,
    row_ref,
    query_sum,
    key_sum,
    value_sum,
):
    seq_len, head_dim = query_ref.shape
    scale = head_dim ** (-0.5)
    length = length_ref[0]
    head = pl.program_id(0)
    place_in_group = lax.rem(head, group_size)

    @pl.when(head == 0)
    def _():
        query_gain_grad_ref[...] = jnp.zeros_like(query_gain_grad_ref)
        key_gain_grad_ref[...] = jnp.zeros_like(key_gain_grad_ref)
        row_ref[...] = jnp.zeros_like(row_ref)

    @pl.when(place_in_group == 0)
    def _():
        key_sum[...] = jnp.zeros_like(key_sum)
        value_sum[...] = jnp.zeros_like(value_sum)

    above = lax.broadcasted_iota(jnp.int32, (block, block), 0) <= lax.broadcasted_iota(
        jnp.int32, (block, block), 1
    )
    for start in range(0, seq_len, block):
        rows = slice(start, start + block)
        queries, grads = query_ref[rows, :], grad_ref[rows, :]
        parts = []
        for first, count in ((0, start), (start, block)):
            if not count:
                continue
            scores = dot(key_ref[first : first + count, :], queries, ((1,), (1,))) * scale
            place = first + lax.broadcasted_iota(jnp.int32, (count, 1), 0)
            scores = jnp.where(place < length, scores, -1e30)
            if first == start:
                scores = jnp.where(above, scores, -1e30)
            parts.append((slice(first, first + count), scores))
        highest = parts[0][1].max(axis=0, keepdims=True)
        for _, scores in parts[1:]:
            highest = jnp.maximum(highest, scores.max(axis=0, keepdims=True))
        parts = [(keys, jnp.exp(scores - highest)) for keys, scores in parts]
        total = sum(raised.sum(axis=0, keepdims=True) for _, raised in parts)
        inverse = 1.0 / total
        centre, weighted = 0.0, []
        for keys, raised in parts:
            weights = raised * inverse
            values = value_raw_ref[keys, :].astype(jnp.bfloat16)
            weight_grad = dot(values, grads, ((1,), (1,)))
            centre = centre + (weights * weight_grad).sum(axis=0, keepdims=True)
            value_sum[keys, :] += dot(weights.astype(jnp.bfloat16), grads, ((1,), (0,)))
            weighted.append((keys, weights, weight_grad))
        query_grad = 0.0
        for keys, weights, weight_grad in weighted:
            score_grad = (weights * (weight_grad - centre)).astype(jnp.bfloat16)
            key_sum[keys, :] += dot(score_grad, queries, ((1,), (0,)))
            query_grad = query_grad + dot(score_grad, key_ref[keys, :], ((0,), (0,)))
        query_sum[rows, :] = query_grad

    def back(total, raw, gain):
        grad = total * scale
        grad = grad * cosine_ref[...] - turn(grad) * sine_ref[...]
        factor = head_factor(raw)
        gain_grad = (grad * raw * factor).sum(axis=0, keepdims=True)
        grad = grad * gain
        shift = (grad * raw).sum(axis=1, keepdims=True) * (factor * factor * factor / head_dim)
        grad = (grad * factor - raw * shift).astype(jnp.bfloat16)
        row_ref[...] += (grad.astype(jnp.float32) * raw).sum(axis=1, keepdims=True)
        return grad, gain_grad

    query_grad_ref[...], gain_grad = back(query_sum[...], query_raw_ref[...], query_gain_ref[...])
    query_gain_grad_ref[...] += gain_grad

    @pl.when(place_in_group == group_size - 1)
    def _():
        key_grad_ref[...], gain_grad = back(key_sum[...], key_raw_ref[...], key_gain_ref[...])
        key_gain_grad_ref[...] += gain_grad
        value_grad = value_sum[...].astype(jnp.bfloat16)
        value_grad_ref[...] = value_grad
        terms = value_grad.astype(jnp.float32) * value_raw_ref[...]
        row_ref[...] += terms.sum(axis=1, keepdims=True)


def attention_specs(seq_len, head_dim, heads, groups):
    size = heads // groups

    def columns(place):
        return pl.BlockSpec((seq_len, head_dim), lambda head: (0, place(head)))

    raw = [
        columns(lambda head: head),
        columns(lambda head: heads + head // size),
        columns(lambda head: heads + groups + head // size),
    ]
    key = columns(lambda head: head // size)
    gain = pl.BlockSpec((1, head_dim), lambda head: (0, 0))
    length = pl.BlockSpec(memory_space=pltpu.SMEM)
    return length, raw, key, gain, columns(lambda head: 0)


def attention(length, raw, query_gain, key_gain, cosine, sine, heads, groups):
    seq_len, head_dim = cosine.shape
    block = math.gcd(256, seq_len)
    count, columns, key, gain, table = attention_specs(seq_len, head_dim, heads, groups)
    pairs = heads * seq_len * (seq_len + block) // 2
    wide = jax.ShapeDtypeStruct((seq_len, heads * head_dim), jnp.bfloat16)
    return pl.pallas_call(
        partial(attention_kernel, heads // groups, block),
        grid=(heads,),
        in_specs=[count, *columns, gain, gain, table, table],
        out_specs=[columns[0], columns[0], key],
        out_shape=[
            wide,
            wide,
            jax.ShapeDtypeStruct((seq_len, groups * head_dim), jnp.bfloat16),
        ],
        compiler_params=pltpu.CompilerParams(vmem_limit_bytes=40 * 1024 * 1024),
        cost_estimate=pl.CostEstimate(
            flops=4 * pairs * head_dim, bytes_accessed=6 * raw.size, transcendentals=pairs
        ),
        name="attention",
    )(length, raw, raw, raw, query_gain, key_gain, cosine, sine)


def attention_back(
    length, queries, keys, raw, grads, query_gain, key_gain, cosine, sine, heads, groups
):
    seq_len, head_dim = cosine.shape
    block = math.gcd(256, seq_len)
    count, columns, key, gain, table = attention_specs(seq_len, head_dim, heads, groups)
    pairs = heads * seq_len * (seq_len + block) // 2
    rows = pltpu.VMEM((seq_len, head_dim), jnp.float32)
    return pl.pallas_call(
        partial(attention_back_kernel, heads // groups, block),
        grid=(heads,),
        in_specs=[count, columns[0], key, *columns, columns[0], gain, gain, table, table],
        out_specs=[
            columns[0],
            key,
            key,
            gain,
            gain,
            pl.BlockSpec((seq_len, 1), lambda head: (0, 0)),
        ],
        out_shape=[
            jax.ShapeDtypeStruct(queries.shape, jnp.bfloat16),
            jax.ShapeDtypeStruct(keys.shape, jnp.bfloat16),
            jax.ShapeDtypeStruct(keys.shape, jnp.bfloat16),
            jax.ShapeDtypeStruct((1, head_dim), jnp.float32),
            jax.ShapeDtypeStruct((1, head_dim), jnp.float32),
            jax.ShapeDtypeStruct((seq_len, 1), jnp.float32),
        ],
        scratch_shapes=[rows, rows, rows],
        compiler_params=pltpu.CompilerParams(vmem_limit_bytes=40 * 1024 * 1024),
        cost_estimate=pl.CostEstimate(
            flops=10 * pairs * head_dim, bytes_accessed=10 * raw.size, transcendentals=pairs
        ),
        name="attention_back",
    )(length, queries, keys, raw, raw, raw, grads, query_gain, key_gain, cosine, sine)


def feed_kernel(branch_steps, own_width, first_half, *refs):
    rank_ref, heads_ref, token_ref, grad_ref, out_ref, gain_ref = refs[:6]
    gate_ref, up_ref, down_ref = refs[6:9]
    refs = refs[9:] if first_half else refs[15:]
    mixed_ref, product_ref, gate_grad_ref, up_grad_ref, own_ref, root_ref = refs[:6]
    mid_ref, mixed_grad_ref, hidden, total, squares, mid = refs[6:]
    step = pl.program_id(0)
    width = out_ref.shape[1]

    @pl.when(step == 0)
    def _():
        squares[...] = jnp.zeros_like(squares)

    @pl.when(step < branch_steps)
    def _():
        part = token_ref[...].astype(jnp.float32) + dot(heads_ref[...], out_ref[...], ((1,), (0,)))
        hidden[:, pl.ds(pl.multiple_of(step * width, width), width)] = part
        squares[...] += (part * part).sum(axis=1, keepdims=True)

    @pl.when(step == branch_steps)
    def _():
        root = lax.rsqrt(squares[...] / hidden.shape[1] + EPSILON)
        root_ref[...] = root
        mixed_ref[...] = (hidden[...] * root * gain_ref[...]).astype(jnp.bfloat16)
        own_start = pl.multiple_of(rank_ref[0] * own_width, own_width)
        own_ref[...] = hidden[:, pl.ds(own_start, own_width)]
        total[...] = jnp.zeros_like(total)
        mid[...] = jnp.zeros_like(mid)

    @pl.when(step >= branch_steps)
    def _():
        gate = dot(mixed_ref[...], gate_ref[...], ((1,), (0,)))
        up = dot(mixed_ref[...], up_ref[...], ((1,), (0,)))
        product_grad = dot(grad_ref[...], down_ref[...], ((1,), (1,)))
        sigmoid = jax.nn.sigmoid(gate)
        activated = gate * sigmoid
        product_ref[...] = (activated * up).astype(jnp.bfloat16)
        slope = sigmoid * (1.0 + gate * (1.0 - sigmoid))
        gate_grad = (product_grad * up * slope).astype(jnp.bfloat16)
        up_grad = (product_grad * activated).astype(jnp.bfloat16)
        gate_grad_ref[...] = gate_grad
        up_grad_ref[...] = up_grad
        terms = gate_grad.astype(jnp.float32) * gate + up_grad.astype(jnp.float32) * up
        mid[...] += terms.sum(axis=1, keepdims=True)
        total[...] += dot(gate_grad, gate_ref[...], ((1,), (1,)))
        total[...] += dot(up_grad, up_ref[...], ((1,), (1,)))

    @pl.when(step == pl.num_programs(0) - 1)
    def _():
        mixed_grad_ref[...] = total[...].astype(jnp.bfloat16)
        mid_ref[...] = mid[...]


def feed_forward(part, earlier, rank, heads, tokens, grads, out_full, gain, gate, up, down, own):
    seq_len, model_width = tokens.shape
    half, hidden_width = seq_len // 2, gate.shape[1]
    wide = math.gcd(512, model_width)
    tile = math.gcd(512, hidden_width)
    branch_steps = model_width // wide
    steps = branch_steps + hidden_width // tile

    def first(step):
        return jnp.minimum(step, branch_steps - 1)

    def second(step):
        return jnp.maximum(step - branch_steps, 0)

    once = pl.Buffered(1)
    f32, bf16 = jnp.float32, jnp.bfloat16
    in_specs = [
        pl.BlockSpec(memory_space=pltpu.SMEM),
        pl.BlockSpec((half, heads.shape[1]), lambda i: (0, 0), pipeline_mode=once),
        pl.BlockSpec((half, wide), lambda i: (part, first(i))),
        pl.BlockSpec((half, model_width), lambda i: (part, 0), pipeline_mode=once),
        pl.BlockSpec((out_full.shape[0], wide), lambda i: (0, first(i))),
        pl.BlockSpec((1, model_width), lambda i: (0, 0)),
        pl.BlockSpec((model_width, tile), lambda i: (0, second(i))),
        pl.BlockSpec((model_width, tile), lambda i: (0, second(i))),
        pl.BlockSpec((tile, model_width), lambda i: (second(i), 0)),
    ]
    in_specs += [pl.BlockSpec(memory_space=pl.ANY)] * len(earlier)
    inner = pl.BlockSpec((half, tile), lambda i: (part, second(i)))
    out_specs = [
        pl.BlockSpec((half, model_width), lambda i: (part, 0), pipeline_mode=once),
        inner,
        inner,
        inner,
        pl.BlockSpec((half, own), lambda i: (part, 0), pipeline_mode=once),
        pl.BlockSpec((half, 1), lambda i: (part, 0), pipeline_mode=once),
        pl.BlockSpec((half, 1), lambda i: (0, 0), pipeline_mode=once),
        pl.BlockSpec((half, model_width), lambda i: (0, 0), pipeline_mode=once),
    ]
    out_shape = [
        jax.ShapeDtypeStruct((seq_len, model_width), bf16),
        jax.ShapeDtypeStruct((seq_len, hidden_width), bf16),
        jax.ShapeDtypeStruct((seq_len, hidden_width), bf16),
        jax.ShapeDtypeStruct((seq_len, hidden_width), bf16),
        jax.ShapeDtypeStruct((seq_len, own), f32),
        jax.ShapeDtypeStruct((seq_len, 1), f32),
        jax.ShapeDtypeStruct((half, 1), f32),
        jax.ShapeDtypeStruct((half, model_width), bf16),
    ]
    return pl.pallas_call(
        partial(feed_kernel, branch_steps, own, not earlier),
        grid=(steps,),
        in_specs=in_specs,
        out_specs=out_specs,
        out_shape=out_shape,
        input_output_aliases={9 + i: i for i in range(len(earlier))},
        scratch_shapes=[
            pltpu.VMEM((half, model_width), f32),
            pltpu.VMEM((half, model_width), f32),
            pltpu.VMEM((half, 1), f32),
            pltpu.VMEM((half, 1), f32),
        ],
        compiler_params=pltpu.CompilerParams(vmem_limit_bytes=58 * 1024 * 1024),
        cost_estimate=pl.CostEstimate(
            flops=2 * half * model_width * (heads.shape[1] + 5 * hidden_width),
            bytes_accessed=2 * (out_full.size + gate.size + up.size + down.size),
            transcendentals=half * hidden_width,
        ),
        name="feed_forward",
    )(rank, heads, tokens, grads, out_full, gain, gate, up, down, *earlier)


def small_sum(values, axis, size):
    total = values
    for shift in range(1, size):
        pairs = [(i, (i + shift) % size) for i in range(size)]
        total = total + lax.ppermute(values, axis, pairs)
    return total


def after(value, *others):
    return lax.optimization_barrier((value, others))[0]


def pair_sum(left, right, core, pairs):
    half = left.shape[1] // 2

    def rows(which):
        part = lax.dynamic_slice_in_dim(left, which * half, half, 1)
        return dot(part, right, ((0,), (0,)))

    received = lax.ppermute(rows(1 - core).astype(jnp.bfloat16), "dp", pairs)
    return (rows(core) + received.astype(jnp.float32)).astype(jnp.bfloat16)


def halving_sum(value, bits, rank, size, gates):
    for bit in bits:
        half = value.shape[0] // 2
        side = lax.rem(rank >> bit, 2)
        pairs = [(i, i ^ (1 << bit)) for i in range(size)]
        sent = lax.dynamic_slice_in_dim(value, (1 - side) * half, half, 0)
        kept = lax.dynamic_slice_in_dim(value, side * half, half, 0).astype(jnp.float32)
        value = (kept + lax.ppermute(sent, "dp", pairs).astype(jnp.float32)).astype(jnp.bfloat16)
    for place, bit in enumerate(reversed(bits)):
        value = after(value, gates[min(place, len(gates) - 1)])
        side = lax.rem(rank >> bit, 2)
        pairs = [(i, i ^ (1 << bit)) for i in range(size)]
        other = lax.ppermute(value, "dp", pairs)
        parts = (jnp.where(side == 0, value, other), jnp.where(side == 0, other, value))
        value = jnp.concatenate(parts, axis=0)
    return value


def chip_sum(value, rank, size, gates):
    bits = list(range(1, size.bit_length() - 1))
    half = value.shape[0] // 2
    parts = (
        halving_sum(value[:half], bits, rank, size, gates),
        halving_sum(value[half:], bits[::-1], rank, size, gates),
    )
    return jnp.concatenate(parts, axis=0)


def join_kernel(steps, core_ref, mine_ref, other_ref, *out_refs):
    own = (pl.program_id(0) < steps) == (core_ref[0] == 0)

    def write(source_ref):
        start = 0
        for out_ref in out_refs:
            width = out_ref.shape[1]
            out_ref[...] = source_ref[:, start : start + width].astype(jnp.float32)
            start += width

    pl.when(own)(lambda: write(mine_ref))
    pl.when(jnp.logical_not(own))(lambda: write(other_ref))


def both_halves(mine, core, pairs, widths):
    other = lax.ppermute(mine, "dp", pairs)
    half, width = mine.shape
    block = math.gcd(256, half)
    steps = half // block

    def place(step, first):
        return jnp.clip(step - jnp.where(first, 0, steps), 0, steps - 1)

    grid_spec = pltpu.PrefetchScalarGridSpec(
        num_scalar_prefetch=1,
        grid=(2 * steps,),
        in_specs=[
            pl.BlockSpec((block, width), lambda i, core_ref: (place(i, core_ref[0] == 0), 0)),
            pl.BlockSpec((block, width), lambda i, core_ref: (place(i, core_ref[0] != 0), 0)),
        ],
        out_specs=[pl.BlockSpec((block, each), lambda i, core_ref: (i, 0)) for each in widths],
    )
    return pl.pallas_call(
        partial(join_kernel, steps),
        grid_spec=grid_spec,
        out_shape=[jax.ShapeDtypeStruct((2 * half, each), jnp.float32) for each in widths],
        compiler_params=pltpu.CompilerParams(vmem_limit_bytes=32 * 1024 * 1024),
        cost_estimate=pl.CostEstimate(
            flops=mine.size, bytes_accessed=12 * mine.size, transcendentals=0
        ),
        name="join",
    )(core.astype(jnp.int32)[None], mine, other)


def local(
    tensor_size,
    dp_size,
    tokens,
    lengths,
    cotangent,
    first_gain,
    query_weight,
    key_weight,
    value_weight,
    query_gain,
    key_gain,
    out_weight,
    second_gain,
    gate_weight,
    up_weight,
    down_weight,
):
    bf16 = jnp.bfloat16
    tensor_rank = lax.axis_index("tensor")
    dp_rank = lax.axis_index("dp")
    seq_len = tokens.shape[0]
    share_width = tokens.shape[1]
    model_width = first_gain.shape[0]
    head_dim = query_gain.shape[0]
    local_heads = query_weight.shape[1] // head_dim
    local_groups = key_weight.shape[1] // head_dim
    length = lengths[0]
    valid_rows = (jnp.arange(seq_len, dtype=jnp.int32) < length).astype(jnp.float32)[:, None]
    own_start = tensor_rank * share_width
    first_own = lax.dynamic_slice_in_dim(first_gain, own_start, share_width, 0)
    second_own = lax.dynamic_slice_in_dim(second_gain, own_start, share_width, 0)
    full_tokens = lax.all_gather(tokens, "tensor", axis=1, tiled=True)
    out_cols = model_width // dp_size
    out_rows = out_weight.shape[0]
    out_part = lax.dynamic_slice_in_dim(out_weight, dp_rank * out_cols, out_cols, 1)
    pieces = [out_part]
    for shift in range(1, tensor_size):
        ring = [(i, (i + shift) % tensor_size) for i in range(tensor_size)]
        pieces.append(lax.ppermute(out_part, "tensor", ring))
    full_tokens = after(full_tokens, *pieces)
    full_cot = lax.all_gather(after(cotangent, full_tokens), "tensor", axis=1, tiled=True)
    out_block = jnp.zeros((out_rows * tensor_size, out_cols), bf16)
    for shift, piece in enumerate(pieces):
        source = lax.rem(tensor_rank + tensor_size - shift, tensor_size)
        out_block = lax.dynamic_update_slice_in_dim(out_block, piece, source * out_rows, 0)
    out_full = jnp.zeros((out_rows * tensor_size, model_width), bf16)
    out_full = lax.dynamic_update_slice_in_dim(out_full, out_block, dp_rank * out_cols, 1)
    rotated_order = [[(i + 1) % dp_size for i in range(dp_size)]]
    out_full = lax.psum(out_full, "dp", axis_index_groups=rotated_order)

    token_own = tokens.astype(jnp.float32)
    token_rows = full_tokens.astype(jnp.float32)
    first_root = lax.rsqrt(jnp.mean(token_rows * token_rows, axis=1, keepdims=True) + EPSILON)
    normed = (token_rows * first_root * first_gain).astype(bf16)
    heads_weight = jnp.concatenate([query_weight, key_weight, value_weight], axis=1)
    raw = dot(normed, heads_weight, ((1,), (0,)))
    cosine, sine = rope_rows(seq_len, head_dim)
    head_gains = (query_gain[None, :], key_gain[None, :])
    counts = (local_heads, local_groups)
    attended, query_rows, key_rows = attention(lengths, raw, *head_gains, cosine, sine, *counts)

    out_full = after(out_full, attended)
    attended = after(attended, full_cot)
    grad_full = (full_cot.astype(jnp.float32) * valid_rows).astype(bf16)
    grad_own = cotangent.astype(jnp.float32) * valid_rows
    out_full = after(out_full, grad_full)

    half = seq_len // 2
    heads_in = (attended[:half], after(attended[half:], out_full))
    heads_parts = [lax.all_gather(part, "tensor", axis=1, tiled=True) for part in heads_in]
    rank = tensor_rank.astype(jnp.int32)[None]
    grad_parts, mid_parts, kept = [], [], []
    for part, heads_full in enumerate(heads_parts):
        *kept, mid, mixed_grad = feed_forward(
            part,
            kept,
            rank,
            heads_full,
            full_tokens,
            grad_full,
            out_full,
            second_gain[None, :],
            gate_weight,
            up_weight,
            down_weight,
            share_width,
        )
        mid_parts.append(small_sum(mid[:, 0], "tensor", tensor_size)[:, None])
        if grad_parts:
            mixed_grad = after(mixed_grad, grad_parts[-1])
        grad_parts.append(lax.psum_scatter(mixed_grad, "tensor", scatter_dimension=1, tiled=True))
    mixed_rows, product, gate_grads, up_grads, hidden_own, second_root = kept
    core = lax.rem(dp_rank, 2)
    pairs = [(i, i ^ 1) for i in range(dp_size)]
    chips = [[i for i in range(dp_size) if i % 2 == side] for side in (0, 1)]
    early = (
        pair_sum(product, grad_full, core, pairs),
        pair_sum(mixed_rows, gate_grads, core, pairs),
        pair_sum(mixed_rows, up_grads, core, pairs),
    )
    down_part = dot(after(product, *early), down_weight, ((1,), (0,))).astype(bf16)
    grad_parts, mid_parts = after((grad_parts, mid_parts), *early)
    mixed_own_grad = jnp.concatenate(grad_parts, axis=0).astype(jnp.float32)
    mid_total = jnp.concatenate(mid_parts, axis=0)
    early = lax.psum(early, "dp", axis_index_groups=chips)

    second_gain_grad = jnp.sum(mixed_own_grad * hidden_own * second_root, axis=0)
    hidden_grad = (
        grad_own
        + mixed_own_grad * second_own * second_root
        - hidden_own * second_root**2 / model_width * mid_total
    )
    hidden_grad_rows = lax.all_gather(hidden_grad.astype(bf16), "tensor", axis=1, tiled=True)
    down_part, hidden_grad_rows = lax.optimization_barrier((down_part, hidden_grad_rows))
    down_own = lax.psum_scatter(down_part, "tensor", scatter_dimension=1, tiled=True)
    attended_grad = dot(hidden_grad_rows, out_weight, ((1,), (1,))).astype(bf16)
    *raw_grads, query_gain_grad, key_gain_grad, row_sum = attention_back(
        lengths, query_rows, key_rows, raw, attended_grad, *head_gains, cosine, sine, *counts
    )
    raw_grad = jnp.concatenate(raw_grads, axis=1)
    row_sum = small_sum(row_sum[:, 0], "tensor", tensor_size)[:, None]
    normed_grad = dot(raw_grad, heads_weight, ((1,), (1,))).astype(bf16)
    normed_own_grad = lax.psum_scatter(normed_grad, "tensor", scatter_dimension=1, tiled=True)
    first_gain_part = jnp.sum(
        normed_grad.astype(jnp.float32) * (full_tokens.astype(jnp.float32) * first_root), axis=0
    )
    second_gain_part = lax.dynamic_update_slice_in_dim(
        jnp.zeros((model_width,), jnp.float32), second_gain_grad, own_start, 0
    )
    gains = [first_gain_part, second_gain_part, query_gain_grad[0], key_gain_grad[0]]
    gains = small_sum(jnp.concatenate(gains), "tensor", tensor_size)
    for bit in range(dp_size.bit_length() - 1):
        gains = gains + lax.ppermute(gains, "dp", [(i, i ^ (1 << bit)) for i in range(dp_size)])
    grad_out = pair_sum(attended, hidden_grad_rows, core, pairs)
    grad_heads = pair_sum(normed, raw_grad, core, pairs)
    early = after(early, grad_out, grad_heads, gains, row_sum)
    down_own = after(down_own, normed_grad, grad_out, grad_heads)
    (grad_down,), (grad_gate,), (grad_up,) = (
        both_halves(part, core, pairs, (part.shape[1],)) for part in early
    )
    gates = (early, grad_down)
    grad_out, grad_heads = (
        chip_sum(after(part, normed_grad), dp_rank, dp_size, gates)
        for part in (grad_out, grad_heads)
    )
    layer_out = (hidden_own + down_own.astype(jnp.float32)).astype(bf16)
    normed_own_grad = after(normed_own_grad, layer_out, gains, *early).astype(jnp.float32)
    token_grad = (
        hidden_grad
        + normed_own_grad * first_own * first_root
        - token_own * first_root**2 / model_width * row_sum
    ).astype(bf16)
    grad_out, grad_heads = after(
        (grad_out, grad_heads), grad_gate, grad_up, layer_out, token_grad
    )
    (grad_out,) = both_halves(grad_out, core, pairs, (model_width,))
    query_width, key_width = query_weight.shape[1], key_weight.shape[1]
    grad_query, grad_key, grad_value = both_halves(
        grad_heads, core, pairs, (query_width, key_width, key_width)
    )
    first_gain_grad = lax.dynamic_slice_in_dim(gains, own_start, share_width, 0)
    second_gain_grad = lax.dynamic_slice_in_dim(gains, model_width + own_start, share_width, 0)
    query_gain_grad = gains[2 * model_width : 2 * model_width + head_dim]
    key_gain_grad = gains[2 * model_width + head_dim :]
    return (
        layer_out,
        token_grad,
        first_gain_grad,
        grad_query,
        grad_key,
        grad_value,
        query_gain_grad,
        key_gain_grad,
        grad_out,
        second_gain_grad,
        grad_gate,
        grad_up,
        grad_down,
    )


def solution(mesh):
    in_specs = (
        P("dp", "tensor"),
        P("dp"),
        P("dp", "tensor"),
        P(),
        P(None, "tensor"),
        P(None, "tensor"),
        P(None, "tensor"),
        P(),
        P(),
        P("tensor", None),
        P(),
        P(None, "tensor"),
        P(None, "tensor"),
        P("tensor", None),
    )
    out_specs = (
        P("dp", "tensor"),
        P("dp", "tensor"),
        P("tensor"),
        P(None, "tensor"),
        P(None, "tensor"),
        P(None, "tensor"),
        P(),
        P(),
        P("tensor", None),
        P("tensor"),
        P(None, "tensor"),
        P(None, "tensor"),
        P("tensor", None),
    )
    return jax.shard_map(
        partial(local, mesh.shape["tensor"], mesh.shape["dp"]), mesh=mesh, in_specs=in_specs, out_specs=out_specs, check_vma=False)
```

```python
import math
from functools import partial

import jax
import jax.numpy as jnp
from jax import lax
from jax.experimental import pallas as pl
from jax.experimental.pallas import tpu as pltpu
from jax.sharding import PartitionSpec as P

EPSILON = 1e-06
ROPE_BASE = 1000000.0


def rope_tables(seq_len, head_dim):
    half_dim = head_dim // 2
    frequency = ROPE_BASE ** (-(jnp.arange(half_dim, dtype=jnp.float32) * 2.0 / head_dim))
    angles = jnp.arange(seq_len, dtype=jnp.float32)[:, None] * frequency[None, :]
    angles = jnp.concatenate([angles, angles], axis=1)
    return (jnp.cos(angles)[:, None, :], jnp.sin(angles)[:, None, :])


def rope_rows(seq_len, head_dim):
    cosine, sine = rope_tables(seq_len, head_dim)
    signs = jnp.where(jnp.arange(head_dim) < head_dim // 2, -1.0, 1.0)
    return cosine[:, 0, :], sine[:, 0, :] * signs[None, :]


def head_factor(raw):
    return lax.rsqrt(jnp.mean(raw * raw, axis=-1, keepdims=True) + EPSILON)


def turn(values):
    return pltpu.roll(values, values.shape[-1] // 2, 1)


def dot(left, right, contract):
    return lax.dot_general(left, right, (contract, ((), ())), preferred_element_type=jnp.float32)


def attention_kernel(
    group_size,
    block,
    length_ref,
    query_ref,
    key_ref,
    value_ref,
    query_gain_ref,
    key_gain_ref,
    cosine_ref,
    sine_ref,
    out_ref,
    query_out_ref,
    key_out_ref,
):
    seq_len, head_dim = query_ref.shape
    scale = head_dim ** (-0.5)
    length = length_ref[0]

    def post(raw, gain):
        normed = raw * head_factor(raw) * gain
        return (normed * cosine_ref[...] + turn(normed) * sine_ref[...]).astype(jnp.bfloat16)

    @pl.when(lax.rem(pl.program_id(0), group_size) == 0)
    def _():
        key_out_ref[...] = post(key_ref[...], key_gain_ref[...])

    query_out_ref[...] = post(query_ref[...], query_gain_ref[...])
    below = lax.broadcasted_iota(jnp.int32, (block, block), 0) >= lax.broadcasted_iota(
        jnp.int32, (block, block), 1
    )
    for start in range(0, seq_len, block):
        queries = query_out_ref[start : start + block, :]
        parts = []
        for first, count in ((0, start), (start, block)):
            if not count:
                continue
            scores = dot(queries, key_out_ref[first : first + count, :], ((1,), (1,))) * scale
            place = first + lax.broadcasted_iota(jnp.int32, (1, count), 1)
            scores = scores + jnp.where(place < length, 0.0, -1e30)
            if first == start:
                scores = jnp.where(below, scores, -1e30)
            parts.append((first, count, scores))
        highest = parts[0][2].max(axis=1, keepdims=True)
        for _, _, scores in parts[1:]:
            highest = jnp.maximum(highest, scores.max(axis=1, keepdims=True))
        total, result = 0.0, 0.0
        for first, count, scores in parts:
            raised = jnp.exp(scores - highest)
            total = total + raised.sum(axis=1, keepdims=True)
            values = value_ref[first : first + count, :].astype(jnp.bfloat16)
            result = result + dot(raised.astype(jnp.bfloat16), values, ((1,), (0,)))
        out_ref[start : start + block, :] = (result / total).astype(jnp.bfloat16)


def attention_back_kernel(
    group_size,
    block,
    length_ref,
    query_ref,
    key_ref,
    query_raw_ref,
    key_raw_ref,
    value_raw_ref,
    grad_ref,
    query_gain_ref,
    key_gain_ref,
    cosine_ref,
    sine_ref,
    query_grad_ref,
    key_grad_ref,
    value_grad_ref,
    query_gain_grad_ref,
    key_gain_grad_ref,
    row_ref,
    query_sum,
    key_sum,
    value_sum,
):
    seq_len, head_dim = query_ref.shape
    scale = head_dim ** (-0.5)
    length = length_ref[0]
    head = pl.program_id(0)
    place_in_group = lax.rem(head, group_size)

    @pl.when(head == 0)
    def _():
        query_gain_grad_ref[...] = jnp.zeros_like(query_gain_grad_ref)
        key_gain_grad_ref[...] = jnp.zeros_like(key_gain_grad_ref)
        row_ref[...] = jnp.zeros_like(row_ref)

    @pl.when(place_in_group == 0)
    def _():
        key_sum[...] = jnp.zeros_like(key_sum)
        value_sum[...] = jnp.zeros_like(value_sum)

    above = lax.broadcasted_iota(jnp.int32, (block, block), 0) <= lax.broadcasted_iota(
        jnp.int32, (block, block), 1
    )
    for start in range(0, seq_len, block):
        rows = slice(start, start + block)
        queries, grads = query_ref[rows, :], grad_ref[rows, :]
        parts = []
        for first, count in ((0, start), (start, block)):
            if not count:
                continue
            scores = dot(key_ref[first : first + count, :], queries, ((1,), (1,))) * scale
            place = first + lax.broadcasted_iota(jnp.int32, (count, 1), 0)
            scores = jnp.where(place < length, scores, -1e30)
            if first == start:
                scores = jnp.where(above, scores, -1e30)
            parts.append((slice(first, first + count), scores))
        highest = parts[0][1].max(axis=0, keepdims=True)
        for _, scores in parts[1:]:
            highest = jnp.maximum(highest, scores.max(axis=0, keepdims=True))
        parts = [(keys, jnp.exp(scores - highest)) for keys, scores in parts]
        total = sum(raised.sum(axis=0, keepdims=True) for _, raised in parts)
        inverse = 1.0 / total
        centre, weighted = 0.0, []
        for keys, raised in parts:
            weights = raised * inverse
            values = value_raw_ref[keys, :].astype(jnp.bfloat16)
            weight_grad = dot(values, grads, ((1,), (1,)))
            centre = centre + (weights * weight_grad).sum(axis=0, keepdims=True)
            value_sum[keys, :] += dot(weights.astype(jnp.bfloat16), grads, ((1,), (0,)))
            weighted.append((keys, weights, weight_grad))
        query_grad = 0.0
        for keys, weights, weight_grad in weighted:
            score_grad = (weights * (weight_grad - centre)).astype(jnp.bfloat16)
            key_sum[keys, :] += dot(score_grad, queries, ((1,), (0,)))
            query_grad = query_grad + dot(score_grad, key_ref[keys, :], ((0,), (0,)))
        query_sum[rows, :] = query_grad

    def back(total, raw, gain):
        grad = total * scale
        grad = grad * cosine_ref[...] - turn(grad) * sine_ref[...]
        factor = head_factor(raw)
        gain_grad = (grad * raw * factor).sum(axis=0, keepdims=True)
        grad = grad * gain
        shift = (grad * raw).sum(axis=1, keepdims=True) * (factor * factor * factor / head_dim)
        grad = (grad * factor - raw * shift).astype(jnp.bfloat16)
        row_ref[...] += (grad.astype(jnp.float32) * raw).sum(axis=1, keepdims=True)
        return grad, gain_grad

    query_grad_ref[...], gain_grad = back(query_sum[...], query_raw_ref[...], query_gain_ref[...])
    query_gain_grad_ref[...] += gain_grad

    @pl.when(place_in_group == group_size - 1)
    def _():
        key_grad_ref[...], gain_grad = back(key_sum[...], key_raw_ref[...], key_gain_ref[...])
        key_gain_grad_ref[...] += gain_grad
        value_grad = value_sum[...].astype(jnp.bfloat16)
        value_grad_ref[...] = value_grad
        terms = value_grad.astype(jnp.float32) * value_raw_ref[...]
        row_ref[...] += terms.sum(axis=1, keepdims=True)


def attention_specs(seq_len, head_dim, heads, groups):
    size = heads // groups

    def columns(place):
        return pl.BlockSpec((seq_len, head_dim), lambda head: (0, place(head)))

    raw = [
        columns(lambda head: head),
        columns(lambda head: heads + head // size),
        columns(lambda head: heads + groups + head // size),
    ]
    key = columns(lambda head: head // size)
    gain = pl.BlockSpec((1, head_dim), lambda head: (0, 0))
    length = pl.BlockSpec(memory_space=pltpu.SMEM)
    return length, raw, key, gain, columns(lambda head: 0)


def attention(length, raw, query_gain, key_gain, cosine, sine, heads, groups):
    seq_len, head_dim = cosine.shape
    block = math.gcd(256, seq_len)
    count, columns, key, gain, table = attention_specs(seq_len, head_dim, heads, groups)
    pairs = heads * seq_len * (seq_len + block) // 2
    wide = jax.ShapeDtypeStruct((seq_len, heads * head_dim), jnp.bfloat16)
    return pl.pallas_call(
        partial(attention_kernel, heads // groups, block),
        grid=(heads,),
        in_specs=[count, *columns, gain, gain, table, table],
        out_specs=[columns[0], columns[0], key],
        out_shape=[
            wide,
            wide,
            jax.ShapeDtypeStruct((seq_len, groups * head_dim), jnp.bfloat16),
        ],
        compiler_params=pltpu.CompilerParams(vmem_limit_bytes=40 * 1024 * 1024),
        cost_estimate=pl.CostEstimate(
            flops=4 * pairs * head_dim, bytes_accessed=6 * raw.size, transcendentals=pairs
        ),
        name="attention",
    )(length, raw, raw, raw, query_gain, key_gain, cosine, sine)


def attention_back(
    length, queries, keys, raw, grads, query_gain, key_gain, cosine, sine, heads, groups
):
    seq_len, head_dim = cosine.shape
    block = math.gcd(256, seq_len)
    count, columns, key, gain, table = attention_specs(seq_len, head_dim, heads, groups)
    pairs = heads * seq_len * (seq_len + block) // 2
    rows = pltpu.VMEM((seq_len, head_dim), jnp.float32)
    return pl.pallas_call(
        partial(attention_back_kernel, heads // groups, block),
        grid=(heads,),
        in_specs=[count, columns[0], key, *columns, columns[0], gain, gain, table, table],
        out_specs=[
            columns[0],
            key,
            key,
            gain,
            gain,
            pl.BlockSpec((seq_len, 1), lambda head: (0, 0)),
        ],
        out_shape=[
            jax.ShapeDtypeStruct(queries.shape, jnp.bfloat16),
            jax.ShapeDtypeStruct(keys.shape, jnp.bfloat16),
            jax.ShapeDtypeStruct(keys.shape, jnp.bfloat16),
            jax.ShapeDtypeStruct((1, head_dim), jnp.float32),
            jax.ShapeDtypeStruct((1, head_dim), jnp.float32),
            jax.ShapeDtypeStruct((seq_len, 1), jnp.float32),
        ],
        scratch_shapes=[rows, rows, rows],
        compiler_params=pltpu.CompilerParams(vmem_limit_bytes=40 * 1024 * 1024),
        cost_estimate=pl.CostEstimate(
            flops=10 * pairs * head_dim, bytes_accessed=10 * raw.size, transcendentals=pairs
        ),
        name="attention_back",
    )(length, queries, keys, raw, raw, raw, grads, query_gain, key_gain, cosine, sine)


def feed_kernel(branch_steps, own_width, first_half, *refs):
    rank_ref, heads_ref, token_ref, grad_ref, out_ref, gain_ref = refs[:6]
    gate_ref, up_ref, down_ref = refs[6:9]
    refs = refs[9:] if first_half else refs[15:]
    mixed_ref, product_ref, gate_grad_ref, up_grad_ref, own_ref, root_ref = refs[:6]
    mid_ref, mixed_grad_ref, hidden, total, squares, mid = refs[6:]
    step = pl.program_id(0)
    width = out_ref.shape[1]

    @pl.when(step == 0)
    def _():
        squares[...] = jnp.zeros_like(squares)

    @pl.when(step < branch_steps)
    def _():
        part = token_ref[...].astype(jnp.float32) + dot(heads_ref[...], out_ref[...], ((1,), (0,)))
        hidden[:, pl.ds(pl.multiple_of(step * width, width), width)] = part
        squares[...] += (part * part).sum(axis=1, keepdims=True)

    @pl.when(step == branch_steps)
    def _():
        root = lax.rsqrt(squares[...] / hidden.shape[1] + EPSILON)
        root_ref[...] = root
        mixed_ref[...] = (hidden[...] * root * gain_ref[...]).astype(jnp.bfloat16)
        own_start = pl.multiple_of(rank_ref[0] * own_width, own_width)
        own_ref[...] = hidden[:, pl.ds(own_start, own_width)]
        total[...] = jnp.zeros_like(total)
        mid[...] = jnp.zeros_like(mid)

    @pl.when(step >= branch_steps)
    def _():
        gate = dot(mixed_ref[...], gate_ref[...], ((1,), (0,)))
        up = dot(mixed_ref[...], up_ref[...], ((1,), (0,)))
        product_grad = dot(grad_ref[...], down_ref[...], ((1,), (1,)))
        sigmoid = jax.nn.sigmoid(gate)
        activated = gate * sigmoid
        product_ref[...] = (activated * up).astype(jnp.bfloat16)
        slope = sigmoid * (1.0 + gate * (1.0 - sigmoid))
        gate_grad = (product_grad * up * slope).astype(jnp.bfloat16)
        up_grad = (product_grad * activated).astype(jnp.bfloat16)
        gate_grad_ref[...] = gate_grad
        up_grad_ref[...] = up_grad
        terms = gate_grad.astype(jnp.float32) * gate + up_grad.astype(jnp.float32) * up
        mid[...] += terms.sum(axis=1, keepdims=True)
        total[...] += dot(gate_grad, gate_ref[...], ((1,), (1,)))
        total[...] += dot(up_grad, up_ref[...], ((1,), (1,)))

    @pl.when(step == pl.num_programs(0) - 1)
    def _():
        mixed_grad_ref[...] = total[...].astype(jnp.bfloat16)
        mid_ref[...] = mid[...]


def feed_forward(part, earlier, rank, heads, tokens, grads, out_full, gain, gate, up, down, own):
    seq_len, model_width = tokens.shape
    half, hidden_width = seq_len // 2, gate.shape[1]
    wide = math.gcd(512, model_width)
    tile = math.gcd(512, hidden_width)
    branch_steps = model_width // wide
    steps = branch_steps + hidden_width // tile

    def first(step):
        return jnp.minimum(step, branch_steps - 1)

    def second(step):
        return jnp.maximum(step - branch_steps, 0)

    once = pl.Buffered(1)
    f32, bf16 = jnp.float32, jnp.bfloat16
    in_specs = [
        pl.BlockSpec(memory_space=pltpu.SMEM),
        pl.BlockSpec((half, heads.shape[1]), lambda i: (0, 0), pipeline_mode=once),
        pl.BlockSpec((half, wide), lambda i: (part, first(i))),
        pl.BlockSpec((half, model_width), lambda i: (part, 0), pipeline_mode=once),
        pl.BlockSpec((out_full.shape[0], wide), lambda i: (0, first(i))),
        pl.BlockSpec((1, model_width), lambda i: (0, 0)),
        pl.BlockSpec((model_width, tile), lambda i: (0, second(i))),
        pl.BlockSpec((model_width, tile), lambda i: (0, second(i))),
        pl.BlockSpec((tile, model_width), lambda i: (second(i), 0)),
    ]
    in_specs += [pl.BlockSpec(memory_space=pl.ANY)] * len(earlier)
    inner = pl.BlockSpec((half, tile), lambda i: (part, second(i)))
    out_specs = [
        pl.BlockSpec((half, model_width), lambda i: (part, 0), pipeline_mode=once),
        inner,
        inner,
        inner,
        pl.BlockSpec((half, own), lambda i: (part, 0), pipeline_mode=once),
        pl.BlockSpec((half, 1), lambda i: (part, 0), pipeline_mode=once),
        pl.BlockSpec((half, 1), lambda i: (0, 0), pipeline_mode=once),
        pl.BlockSpec((half, model_width), lambda i: (0, 0), pipeline_mode=once),
    ]
    out_shape = [
        jax.ShapeDtypeStruct((seq_len, model_width), bf16),
        jax.ShapeDtypeStruct((seq_len, hidden_width), bf16),
        jax.ShapeDtypeStruct((seq_len, hidden_width), bf16),
        jax.ShapeDtypeStruct((seq_len, hidden_width), bf16),
        jax.ShapeDtypeStruct((seq_len, own), f32),
        jax.ShapeDtypeStruct((seq_len, 1), f32),
        jax.ShapeDtypeStruct((half, 1), f32),
        jax.ShapeDtypeStruct((half, model_width), bf16),
    ]
    return pl.pallas_call(
        partial(feed_kernel, branch_steps, own, not earlier),
        grid=(steps,),
        in_specs=in_specs,
        out_specs=out_specs,
        out_shape=out_shape,
        input_output_aliases={9 + i: i for i in range(len(earlier))},
        scratch_shapes=[
            pltpu.VMEM((half, model_width), f32),
            pltpu.VMEM((half, model_width), f32),
            pltpu.VMEM((half, 1), f32),
            pltpu.VMEM((half, 1), f32),
        ],
        compiler_params=pltpu.CompilerParams(vmem_limit_bytes=58 * 1024 * 1024),
        cost_estimate=pl.CostEstimate(
            flops=2 * half * model_width * (heads.shape[1] + 5 * hidden_width),
            bytes_accessed=2 * (out_full.size + gate.size + up.size + down.size),
            transcendentals=half * hidden_width,
        ),
        name="feed_forward",
    )(rank, heads, tokens, grads, out_full, gain, gate, up, down, *earlier)


def small_sum(values, axis, size):
    total = values
    for shift in range(1, size):
        pairs = [(i, (i + shift) % size) for i in range(size)]
        total = total + lax.ppermute(values, axis, pairs)
    return total


def after(value, *others):
    return lax.optimization_barrier((value, others))[0]


def pair_sum(left, right, core, pairs):
    half = left.shape[1] // 2

    def rows(which):
        part = lax.dynamic_slice_in_dim(left, which * half, half, 1)
        return dot(part, right, ((0,), (0,)))

    received = lax.ppermute(rows(1 - core).astype(jnp.bfloat16), "dp", pairs)
    return (rows(core) + received.astype(jnp.float32)).astype(jnp.bfloat16)


def halving_sum(value, bits, rank, size, gates):
    for bit in bits:
        half = value.shape[0] // 2
        side = lax.rem(rank >> bit, 2)
        pairs = [(i, i ^ (1 << bit)) for i in range(size)]
        sent = lax.dynamic_slice_in_dim(value, (1 - side) * half, half, 0)
        kept = lax.dynamic_slice_in_dim(value, side * half, half, 0).astype(jnp.float32)
        value = (kept + lax.ppermute(sent, "dp", pairs).astype(jnp.float32)).astype(jnp.bfloat16)
    for place, bit in enumerate(reversed(bits)):
        value = after(value, gates[min(place, len(gates) - 1)])
        side = lax.rem(rank >> bit, 2)
        pairs = [(i, i ^ (1 << bit)) for i in range(size)]
        other = lax.ppermute(value, "dp", pairs)
        parts = (jnp.where(side == 0, value, other), jnp.where(side == 0, other, value))
        value = jnp.concatenate(parts, axis=0)
    return value


def chip_sum(value, rank, size, gates):
    bits = list(range(1, size.bit_length() - 1))
    half = value.shape[0] // 2
    parts = (
        halving_sum(value[:half], bits, rank, size, gates),
        halving_sum(value[half:], bits[::-1], rank, size, gates),
    )
    return jnp.concatenate(parts, axis=0)


def join_kernel(steps, core_ref, mine_ref, other_ref, *out_refs):
    own = (pl.program_id(0) < steps) == (core_ref[0] == 0)

    def write(source_ref):
        start = 0
        for out_ref in out_refs:
            width = out_ref.shape[1]
            out_ref[...] = source_ref[:, start : start + width].astype(jnp.float32)
            start += width

    pl.when(own)(lambda: write(mine_ref))
    pl.when(jnp.logical_not(own))(lambda: write(other_ref))


def both_halves(mine, core, pairs, widths):
    other = lax.ppermute(mine, "dp", pairs)
    half, width = mine.shape
    block = math.gcd(256, half)
    steps = half // block

    def place(step, first):
        return jnp.clip(step - jnp.where(first, 0, steps), 0, steps - 1)

    grid_spec = pltpu.PrefetchScalarGridSpec(
        num_scalar_prefetch=1,
        grid=(2 * steps,),
        in_specs=[
            pl.BlockSpec((block, width), lambda i, core_ref: (place(i, core_ref[0] == 0), 0)),
            pl.BlockSpec((block, width), lambda i, core_ref: (place(i, core_ref[0] != 0), 0)),
        ],
        out_specs=[pl.BlockSpec((block, each), lambda i, core_ref: (i, 0)) for each in widths],
    )
    return pl.pallas_call(
        partial(join_kernel, steps),
        grid_spec=grid_spec,
        out_shape=[jax.ShapeDtypeStruct((2 * half, each), jnp.float32) for each in widths],
        compiler_params=pltpu.CompilerParams(vmem_limit_bytes=32 * 1024 * 1024),
        cost_estimate=pl.CostEstimate(
            flops=mine.size, bytes_accessed=12 * mine.size, transcendentals=0
        ),
        name="join",
    )(core.astype(jnp.int32)[None], mine, other)


def local(
    tensor_size,
    dp_size,
    tokens,
    lengths,
    cotangent,
    first_gain,
    query_weight,
    key_weight,
    value_weight,
    query_gain,
    key_gain,
    out_weight,
    second_gain,
    gate_weight,
    up_weight,
    down_weight,
):
    bf16 = jnp.bfloat16
    tensor_rank = lax.axis_index("tensor")
    dp_rank = lax.axis_index("dp")
    seq_len = tokens.shape[0]
    share_width = tokens.shape[1]
    model_width = first_gain.shape[0]
    head_dim = query_gain.shape[0]
    local_heads = query_weight.shape[1] // head_dim
    local_groups = key_weight.shape[1] // head_dim
    length = lengths[0]
    valid_rows = (jnp.arange(seq_len, dtype=jnp.int32) < length).astype(jnp.float32)[:, None]
    own_start = tensor_rank * share_width
    first_own = lax.dynamic_slice_in_dim(first_gain, own_start, share_width, 0)
    second_own = lax.dynamic_slice_in_dim(second_gain, own_start, share_width, 0)
    full_tokens = lax.all_gather(tokens, "tensor", axis=1, tiled=True)
    out_cols = model_width // dp_size
    out_rows = out_weight.shape[0]
    out_part = lax.dynamic_slice_in_dim(out_weight, dp_rank * out_cols, out_cols, 1)
    pieces = [out_part]
    for shift in range(1, tensor_size):
        ring = [(i, (i + shift) % tensor_size) for i in range(tensor_size)]
        pieces.append(lax.ppermute(out_part, "tensor", ring))
    full_tokens = after(full_tokens, *pieces)
    full_cot = lax.all_gather(after(cotangent, full_tokens), "tensor", axis=1, tiled=True)
    out_block = jnp.zeros((out_rows * tensor_size, out_cols), bf16)
    for shift, piece in enumerate(pieces):
        source = lax.rem(tensor_rank + tensor_size - shift, tensor_size)
        out_block = lax.dynamic_update_slice_in_dim(out_block, piece, source * out_rows, 0)
    out_full = jnp.zeros((out_rows * tensor_size, model_width), bf16)
    out_full = lax.dynamic_update_slice_in_dim(out_full, out_block, dp_rank * out_cols, 1)
    rotated_order = [[(i + 1) % dp_size for i in range(dp_size)]]
    out_full = lax.psum(out_full, "dp", axis_index_groups=rotated_order)

    token_own = tokens.astype(jnp.float32)
    token_rows = full_tokens.astype(jnp.float32)
    first_root = lax.rsqrt(jnp.mean(token_rows * token_rows, axis=1, keepdims=True) + EPSILON)
    normed = (token_rows * first_root * first_gain).astype(bf16)
    heads_weight = jnp.concatenate([query_weight, key_weight, value_weight], axis=1)
    raw = dot(normed, heads_weight, ((1,), (0,)))
    cosine, sine = rope_rows(seq_len, head_dim)
    head_gains = (query_gain[None, :], key_gain[None, :])
    counts = (local_heads, local_groups)
    attended, query_rows, key_rows = attention(lengths, raw, *head_gains, cosine, sine, *counts)

    out_full = after(out_full, attended)
    attended = after(attended, full_cot)
    grad_full = (full_cot.astype(jnp.float32) * valid_rows).astype(bf16)
    grad_own = cotangent.astype(jnp.float32) * valid_rows
    out_full = after(out_full, grad_full)

    half = seq_len // 2
    heads_in = (attended[:half], after(attended[half:], grad_full))
    heads_parts = [lax.all_gather(part, "tensor", axis=1, tiled=True) for part in heads_in]
    rank = tensor_rank.astype(jnp.int32)[None]
    grad_parts, mid_parts, kept = [], [], []
    for part, heads_full in enumerate(heads_parts):
        *kept, mid, mixed_grad = feed_forward(
            part,
            kept,
            rank,
            heads_full,
            full_tokens,
            grad_full,
            out_full,
            second_gain[None, :],
            gate_weight,
            up_weight,
            down_weight,
            share_width,
        )
        mid_parts.append(mid[:, 0])
        if grad_parts:
            mixed_grad = after(mixed_grad, grad_parts[-1])
        grad_parts.append(lax.psum_scatter(mixed_grad, "tensor", scatter_dimension=1, tiled=True))
    mixed_rows, product, gate_grads, up_grads, hidden_own, second_root = kept
    core = lax.rem(dp_rank, 2)
    pairs = [(i, i ^ 1) for i in range(dp_size)]
    chips = [[i for i in range(dp_size) if i % 2 == side] for side in (0, 1)]
    early = (
        pair_sum(product, grad_full, core, pairs),
        pair_sum(mixed_rows, gate_grads, core, pairs),
        pair_sum(mixed_rows, up_grads, core, pairs),
    )
    down_part = dot(after(product, *early), down_weight, ((1,), (0,))).astype(bf16)
    mid_total = small_sum(jnp.concatenate(mid_parts), "tensor", tensor_size)[:, None]
    grad_parts, mid_total = after((grad_parts, mid_total), *early)
    mixed_own_grad = jnp.concatenate(grad_parts, axis=0).astype(jnp.float32)
    early = lax.psum(early, "dp", axis_index_groups=chips)

    second_gain_grad = jnp.sum(mixed_own_grad * hidden_own * second_root, axis=0)
    hidden_grad = (
        grad_own
        + mixed_own_grad * second_own * second_root
        - hidden_own * second_root**2 / model_width * mid_total
    )
    hidden_grad_rows = lax.all_gather(hidden_grad.astype(bf16), "tensor", axis=1, tiled=True)
    down_part, hidden_grad_rows = lax.optimization_barrier((down_part, hidden_grad_rows))
    down_own = lax.psum_scatter(down_part, "tensor", scatter_dimension=1, tiled=True)
    attended_grad = dot(hidden_grad_rows, out_weight, ((1,), (1,))).astype(bf16)
    *raw_grads, query_gain_grad, key_gain_grad, row_sum = attention_back(
        lengths, query_rows, key_rows, raw, attended_grad, *head_gains, cosine, sine, *counts
    )
    raw_grad = jnp.concatenate(raw_grads, axis=1)
    row_sum = small_sum(row_sum[:, 0], "tensor", tensor_size)[:, None]
    normed_grad = dot(raw_grad, heads_weight, ((1,), (1,))).astype(bf16)
    normed_own_grad = lax.psum_scatter(normed_grad, "tensor", scatter_dimension=1, tiled=True)
    first_gain_part = jnp.sum(
        normed_grad.astype(jnp.float32) * (full_tokens.astype(jnp.float32) * first_root), axis=0
    )
    second_gain_part = lax.dynamic_update_slice_in_dim(
        jnp.zeros((model_width,), jnp.float32), second_gain_grad, own_start, 0
    )
    gains = [first_gain_part, second_gain_part, query_gain_grad[0], key_gain_grad[0]]
    gains = small_sum(jnp.concatenate(gains), "tensor", tensor_size)
    for bit in range(dp_size.bit_length() - 1):
        gains = gains + lax.ppermute(gains, "dp", [(i, i ^ (1 << bit)) for i in range(dp_size)])
    grad_out = pair_sum(attended, hidden_grad_rows, core, pairs)
    grad_heads = pair_sum(normed, raw_grad, core, pairs)
    early = after(early, grad_out, grad_heads, gains, row_sum)
    down_own = after(down_own, normed_grad, grad_out, grad_heads)
    (grad_down,), (grad_gate,), (grad_up,) = (
        both_halves(part, core, pairs, (part.shape[1],)) for part in early
    )
    gates = (early, grad_down)
    grad_out, grad_heads = (
        chip_sum(after(part, normed_grad), dp_rank, dp_size, gates)
        for part in (grad_out, grad_heads)
    )
    layer_out = (hidden_own + down_own.astype(jnp.float32)).astype(bf16)
    normed_own_grad = after(normed_own_grad, layer_out, gains, *early).astype(jnp.float32)
    token_grad = (
        hidden_grad
        + normed_own_grad * first_own * first_root
        - token_own * first_root**2 / model_width * row_sum
    ).astype(bf16)
    grad_out, grad_heads = after(
        (grad_out, grad_heads), grad_gate, grad_up, layer_out, token_grad
    )
    (grad_out,) = both_halves(grad_out, core, pairs, (model_width,))
    query_width, key_width = query_weight.shape[1], key_weight.shape[1]
    grad_query, grad_key, grad_value = both_halves(
        grad_heads, core, pairs, (query_width, key_width, key_width)
    )
    first_gain_grad = lax.dynamic_slice_in_dim(gains, own_start, share_width, 0)
    second_gain_grad = lax.dynamic_slice_in_dim(gains, model_width + own_start, share_width, 0)
    query_gain_grad = gains[2 * model_width : 2 * model_width + head_dim]
    key_gain_grad = gains[2 * model_width + head_dim :]
    return (
        layer_out,
        token_grad,
        first_gain_grad,
        grad_query,
        grad_key,
        grad_value,
        query_gain_grad,
        key_gain_grad,
        grad_out,
        second_gain_grad,
        grad_gate,
        grad_up,
        grad_down,
    )


def solution(mesh):
    in_specs = (
        P("dp", "tensor"),
        P("dp"),
        P("dp", "tensor"),
        P(),
        P(None, "tensor"),
        P(None, "tensor"),
        P(None, "tensor"),
        P(),
        P(),
        P("tensor", None),
        P(),
        P(None, "tensor"),
        P(None, "tensor"),
        P("tensor", None),
    )
    out_specs = (
        P("dp", "tensor"),
        P("dp", "tensor"),
        P("tensor"),
        P(None, "tensor"),
        P(None, "tensor"),
        P(None, "tensor"),
        P(),
        P(),
        P("tensor", None),
        P("tensor"),
        P(None, "tensor"),
        P(None, "tensor"),
        P("tensor", None),
    )
    return jax.shard_map(
        partial(local, mesh.shape["tensor"], mesh.shape["dp"]), mesh=mesh, in_specs=in_specs, out_specs=out_specs, check_vma=False)
```

```python
import math
from functools import partial

import jax
import jax.numpy as jnp
from jax import lax
from jax.experimental import pallas as pl
from jax.experimental.pallas import tpu as pltpu
from jax.sharding import PartitionSpec as P

EPSILON = 1e-06
ROPE_BASE = 1000000.0


def rope_tables(seq_len, head_dim):
    half_dim = head_dim // 2
    frequency = ROPE_BASE ** (-(jnp.arange(half_dim, dtype=jnp.float32) * 2.0 / head_dim))
    angles = jnp.arange(seq_len, dtype=jnp.float32)[:, None] * frequency[None, :]
    angles = jnp.concatenate([angles, angles], axis=1)
    return (jnp.cos(angles)[:, None, :], jnp.sin(angles)[:, None, :])


def rope_rows(seq_len, head_dim):
    cosine, sine = rope_tables(seq_len, head_dim)
    signs = jnp.where(jnp.arange(head_dim) < head_dim // 2, -1.0, 1.0)
    return cosine[:, 0, :], sine[:, 0, :] * signs[None, :]


def head_factor(raw):
    return lax.rsqrt(jnp.mean(raw * raw, axis=-1, keepdims=True) + EPSILON)


def turn(values):
    return pltpu.roll(values, values.shape[-1] // 2, 1)


def dot(left, right, contract):
    return lax.dot_general(left, right, (contract, ((), ())), preferred_element_type=jnp.float32)


def attention_kernel(
    group_size,
    block,
    length_ref,
    query_ref,
    key_ref,
    value_ref,
    query_gain_ref,
    key_gain_ref,
    cosine_ref,
    sine_ref,
    out_ref,
    query_out_ref,
    key_out_ref,
):
    seq_len, head_dim = query_ref.shape
    scale = head_dim ** (-0.5)
    length = length_ref[0]

    def post(raw, gain):
        normed = raw * head_factor(raw) * gain
        return (normed * cosine_ref[...] + turn(normed) * sine_ref[...]).astype(jnp.bfloat16)

    @pl.when(lax.rem(pl.program_id(0), group_size) == 0)
    def _():
        key_out_ref[...] = post(key_ref[...], key_gain_ref[...])

    query_out_ref[...] = post(query_ref[...], query_gain_ref[...])
    below = lax.broadcasted_iota(jnp.int32, (block, block), 0) >= lax.broadcasted_iota(
        jnp.int32, (block, block), 1
    )
    for start in range(0, seq_len, block):
        queries = query_out_ref[start : start + block, :]
        parts = []
        for first, count in ((0, start), (start, block)):
            if not count:
                continue
            scores = dot(queries, key_out_ref[first : first + count, :], ((1,), (1,))) * scale
            place = first + lax.broadcasted_iota(jnp.int32, (1, count), 1)
            scores = scores + jnp.where(place < length, 0.0, -1e30)
            if first == start:
                scores = jnp.where(below, scores, -1e30)
            parts.append((first, count, scores))
        highest = parts[0][2].max(axis=1, keepdims=True)
        for _, _, scores in parts[1:]:
            highest = jnp.maximum(highest, scores.max(axis=1, keepdims=True))
        total, result = 0.0, 0.0
        for first, count, scores in parts:
            raised = jnp.exp(scores - highest)
            total = total + raised.sum(axis=1, keepdims=True)
            values = value_ref[first : first + count, :].astype(jnp.bfloat16)
            result = result + dot(raised.astype(jnp.bfloat16), values, ((1,), (0,)))
        out_ref[start : start + block, :] = (result / total).astype(jnp.bfloat16)


def attention_back_kernel(
    group_size,
    block,
    length_ref,
    query_ref,
    key_ref,
    query_raw_ref,
    key_raw_ref,
    value_raw_ref,
    grad_ref,
    query_gain_ref,
    key_gain_ref,
    cosine_ref,
    sine_ref,
    query_grad_ref,
    key_grad_ref,
    value_grad_ref,
    query_gain_grad_ref,
    key_gain_grad_ref,
    row_ref,
    query_sum,
    key_sum,
    value_sum,
):
    seq_len, head_dim = query_ref.shape
    scale = head_dim ** (-0.5)
    length = length_ref[0]
    head = pl.program_id(0)
    place_in_group = lax.rem(head, group_size)

    @pl.when(head == 0)
    def _():
        query_gain_grad_ref[...] = jnp.zeros_like(query_gain_grad_ref)
        key_gain_grad_ref[...] = jnp.zeros_like(key_gain_grad_ref)
        row_ref[...] = jnp.zeros_like(row_ref)

    @pl.when(place_in_group == 0)
    def _():
        key_sum[...] = jnp.zeros_like(key_sum)
        value_sum[...] = jnp.zeros_like(value_sum)

    above = lax.broadcasted_iota(jnp.int32, (block, block), 0) <= lax.broadcasted_iota(
        jnp.int32, (block, block), 1
    )
    for start in range(0, seq_len, block):
        rows = slice(start, start + block)
        queries, grads = query_ref[rows, :], grad_ref[rows, :]
        parts = []
        for first, count in ((0, start), (start, block)):
            if not count:
                continue
            scores = dot(key_ref[first : first + count, :], queries, ((1,), (1,))) * scale
            place = first + lax.broadcasted_iota(jnp.int32, (count, 1), 0)
            scores = jnp.where(place < length, scores, -1e30)
            if first == start:
                scores = jnp.where(above, scores, -1e30)
            parts.append((slice(first, first + count), scores))
        highest = parts[0][1].max(axis=0, keepdims=True)
        for _, scores in parts[1:]:
            highest = jnp.maximum(highest, scores.max(axis=0, keepdims=True))
        parts = [(keys, jnp.exp(scores - highest)) for keys, scores in parts]
        total = sum(raised.sum(axis=0, keepdims=True) for _, raised in parts)
        inverse = 1.0 / total
        centre, weighted = 0.0, []
        for keys, raised in parts:
            weights = raised * inverse
            values = value_raw_ref[keys, :].astype(jnp.bfloat16)
            weight_grad = dot(values, grads, ((1,), (1,)))
            centre = centre + (weights * weight_grad).sum(axis=0, keepdims=True)
            value_sum[keys, :] += dot(weights.astype(jnp.bfloat16), grads, ((1,), (0,)))
            weighted.append((keys, weights, weight_grad))
        query_grad = 0.0
        for keys, weights, weight_grad in weighted:
            score_grad = (weights * (weight_grad - centre)).astype(jnp.bfloat16)
            key_sum[keys, :] += dot(score_grad, queries, ((1,), (0,)))
            query_grad = query_grad + dot(score_grad, key_ref[keys, :], ((0,), (0,)))
        query_sum[rows, :] = query_grad

    def back(total, raw, gain):
        grad = total * scale
        grad = grad * cosine_ref[...] - turn(grad) * sine_ref[...]
        factor = head_factor(raw)
        gain_grad = (grad * raw * factor).sum(axis=0, keepdims=True)
        grad = grad * gain
        shift = (grad * raw).sum(axis=1, keepdims=True) * (factor * factor * factor / head_dim)
        grad = (grad * factor - raw * shift).astype(jnp.bfloat16)
        row_ref[...] += (grad.astype(jnp.float32) * raw).sum(axis=1, keepdims=True)
        return grad, gain_grad

    query_grad_ref[...], gain_grad = back(query_sum[...], query_raw_ref[...], query_gain_ref[...])
    query_gain_grad_ref[...] += gain_grad

    @pl.when(place_in_group == group_size - 1)
    def _():
        key_grad_ref[...], gain_grad = back(key_sum[...], key_raw_ref[...], key_gain_ref[...])
        key_gain_grad_ref[...] += gain_grad
        value_grad = value_sum[...].astype(jnp.bfloat16)
        value_grad_ref[...] = value_grad
        terms = value_grad.astype(jnp.float32) * value_raw_ref[...]
        row_ref[...] += terms.sum(axis=1, keepdims=True)


def attention_specs(seq_len, head_dim, heads, groups):
    size = heads // groups

    def columns(place):
        return pl.BlockSpec((seq_len, head_dim), lambda head: (0, place(head)))

    raw = [
        columns(lambda head: head),
        columns(lambda head: heads + head // size),
        columns(lambda head: heads + groups + head // size),
    ]
    key = columns(lambda head: head // size)
    gain = pl.BlockSpec((1, head_dim), lambda head: (0, 0))
    length = pl.BlockSpec(memory_space=pltpu.SMEM)
    return length, raw, key, gain, columns(lambda head: 0)


def attention(length, raw, query_gain, key_gain, cosine, sine, heads, groups):
    seq_len, head_dim = cosine.shape
    block = math.gcd(256, seq_len)
    count, columns, key, gain, table = attention_specs(seq_len, head_dim, heads, groups)
    pairs = heads * seq_len * (seq_len + block) // 2
    wide = jax.ShapeDtypeStruct((seq_len, heads * head_dim), jnp.bfloat16)
    return pl.pallas_call(
        partial(attention_kernel, heads // groups, block),
        grid=(heads,),
        in_specs=[count, *columns, gain, gain, table, table],
        out_specs=[columns[0], columns[0], key],
        out_shape=[
            wide,
            wide,
            jax.ShapeDtypeStruct((seq_len, groups * head_dim), jnp.bfloat16),
        ],
        compiler_params=pltpu.CompilerParams(vmem_limit_bytes=24 * 1024 * 1024),
        cost_estimate=pl.CostEstimate(
            flops=4 * pairs * head_dim, bytes_accessed=6 * raw.size, transcendentals=pairs
        ),
        name="attention",
    )(length, raw, raw, raw, query_gain, key_gain, cosine, sine)


def attention_back(
    length, queries, keys, raw, grads, query_gain, key_gain, cosine, sine, heads, groups
):
    seq_len, head_dim = cosine.shape
    block = math.gcd(256, seq_len)
    count, columns, key, gain, table = attention_specs(seq_len, head_dim, heads, groups)
    pairs = heads * seq_len * (seq_len + block) // 2
    rows = pltpu.VMEM((seq_len, head_dim), jnp.float32)
    return pl.pallas_call(
        partial(attention_back_kernel, heads // groups, block),
        grid=(heads,),
        in_specs=[count, columns[0], key, *columns, columns[0], gain, gain, table, table],
        out_specs=[
            columns[0],
            key,
            key,
            gain,
            gain,
            pl.BlockSpec((seq_len, 1), lambda head: (0, 0)),
        ],
        out_shape=[
            jax.ShapeDtypeStruct(queries.shape, jnp.bfloat16),
            jax.ShapeDtypeStruct(keys.shape, jnp.bfloat16),
            jax.ShapeDtypeStruct(keys.shape, jnp.bfloat16),
            jax.ShapeDtypeStruct((1, head_dim), jnp.float32),
            jax.ShapeDtypeStruct((1, head_dim), jnp.float32),
            jax.ShapeDtypeStruct((seq_len, 1), jnp.float32),
        ],
        scratch_shapes=[rows, rows, rows],
        compiler_params=pltpu.CompilerParams(vmem_limit_bytes=24 * 1024 * 1024),
        cost_estimate=pl.CostEstimate(
            flops=10 * pairs * head_dim, bytes_accessed=10 * raw.size, transcendentals=pairs
        ),
        name="attention_back",
    )(length, queries, keys, raw, raw, raw, grads, query_gain, key_gain, cosine, sine)


def feed_kernel(branch_steps, own_width, first_half, *refs):
    rank_ref, heads_ref, token_ref, grad_ref, out_ref, gain_ref = refs[:6]
    gate_ref, up_ref, down_ref = refs[6:9]
    refs = refs[9:] if first_half else refs[15:]
    mixed_ref, product_ref, gate_grad_ref, up_grad_ref, own_ref, root_ref = refs[:6]
    mid_ref, mixed_grad_ref, hidden, total, squares, mid = refs[6:]
    step = pl.program_id(0)
    width = out_ref.shape[1]

    @pl.when(step == 0)
    def _():
        squares[...] = jnp.zeros_like(squares)

    @pl.when(step < branch_steps)
    def _():
        part = token_ref[...].astype(jnp.float32) + dot(heads_ref[...], out_ref[...], ((1,), (0,)))
        hidden[:, pl.ds(pl.multiple_of(step * width, width), width)] = part
        squares[...] += (part * part).sum(axis=1, keepdims=True)

    @pl.when(step == branch_steps)
    def _():
        root = lax.rsqrt(squares[...] / hidden.shape[1] + EPSILON)
        root_ref[...] = root
        mixed_ref[...] = (hidden[...] * root * gain_ref[...]).astype(jnp.bfloat16)
        own_start = pl.multiple_of(rank_ref[0] * own_width, own_width)
        own_ref[...] = hidden[:, pl.ds(own_start, own_width)]
        total[...] = jnp.zeros_like(total)
        mid[...] = jnp.zeros_like(mid)

    @pl.when(step >= branch_steps)
    def _():
        gate = dot(mixed_ref[...], gate_ref[...], ((1,), (0,)))
        up = dot(mixed_ref[...], up_ref[...], ((1,), (0,)))
        product_grad = dot(grad_ref[...], down_ref[...], ((1,), (1,)))
        sigmoid = jax.nn.sigmoid(gate)
        activated = gate * sigmoid
        product_ref[...] = (activated * up).astype(jnp.bfloat16)
        slope = sigmoid * (1.0 + gate * (1.0 - sigmoid))
        gate_grad = (product_grad * up * slope).astype(jnp.bfloat16)
        up_grad = (product_grad * activated).astype(jnp.bfloat16)
        gate_grad_ref[...] = gate_grad
        up_grad_ref[...] = up_grad
        terms = gate_grad.astype(jnp.float32) * gate + up_grad.astype(jnp.float32) * up
        mid[...] += terms.sum(axis=1, keepdims=True)
        total[...] += dot(gate_grad, gate_ref[...], ((1,), (1,)))
        total[...] += dot(up_grad, up_ref[...], ((1,), (1,)))

    @pl.when(step == pl.num_programs(0) - 1)
    def _():
        mixed_grad_ref[...] = total[...].astype(jnp.bfloat16)
        mid_ref[...] = mid[...]


def feed_forward(part, earlier, rank, heads, tokens, grads, out_full, gain, gate, up, down, own):
    seq_len, model_width = tokens.shape
    half, hidden_width = seq_len // 2, gate.shape[1]
    wide = math.gcd(512, model_width)
    tile = math.gcd(512, hidden_width)
    branch_steps = model_width // wide
    steps = branch_steps + hidden_width // tile

    def first(step):
        return jnp.minimum(step, branch_steps - 1)

    def second(step):
        return jnp.maximum(step - branch_steps, 0)

    once = pl.Buffered(1)
    f32, bf16 = jnp.float32, jnp.bfloat16
    in_specs = [
        pl.BlockSpec(memory_space=pltpu.SMEM),
        pl.BlockSpec((half, heads.shape[1]), lambda i: (0, 0), pipeline_mode=once),
        pl.BlockSpec((half, wide), lambda i: (part, first(i))),
        pl.BlockSpec((half, model_width), lambda i: (part, 0), pipeline_mode=once),
        pl.BlockSpec((out_full.shape[0], wide), lambda i: (0, first(i))),
        pl.BlockSpec((1, model_width), lambda i: (0, 0)),
        pl.BlockSpec((model_width, tile), lambda i: (0, second(i))),
        pl.BlockSpec((model_width, tile), lambda i: (0, second(i))),
        pl.BlockSpec((tile, model_width), lambda i: (second(i), 0)),
    ]
    in_specs += [pl.BlockSpec(memory_space=pl.ANY)] * len(earlier)
    inner = pl.BlockSpec((half, tile), lambda i: (part, second(i)))
    out_specs = [
        pl.BlockSpec((half, model_width), lambda i: (part, 0), pipeline_mode=once),
        inner,
        inner,
        inner,
        pl.BlockSpec((half, own), lambda i: (part, 0), pipeline_mode=once),
        pl.BlockSpec((half, 1), lambda i: (part, 0), pipeline_mode=once),
        pl.BlockSpec((half, 1), lambda i: (0, 0), pipeline_mode=once),
        pl.BlockSpec((half, model_width), lambda i: (0, 0), pipeline_mode=once),
    ]
    out_shape = [
        jax.ShapeDtypeStruct((seq_len, model_width), bf16),
        jax.ShapeDtypeStruct((seq_len, hidden_width), bf16),
        jax.ShapeDtypeStruct((seq_len, hidden_width), bf16),
        jax.ShapeDtypeStruct((seq_len, hidden_width), bf16),
        jax.ShapeDtypeStruct((seq_len, own), f32),
        jax.ShapeDtypeStruct((seq_len, 1), f32),
        jax.ShapeDtypeStruct((half, 1), f32),
        jax.ShapeDtypeStruct((half, model_width), bf16),
    ]
    return pl.pallas_call(
        partial(feed_kernel, branch_steps, own, not earlier),
        grid=(steps,),
        in_specs=in_specs,
        out_specs=out_specs,
        out_shape=out_shape,
        input_output_aliases={9 + i: i for i in range(len(earlier))},
        scratch_shapes=[
            pltpu.VMEM((half, model_width), f32),
            pltpu.VMEM((half, model_width), f32),
            pltpu.VMEM((half, 1), f32),
            pltpu.VMEM((half, 1), f32),
        ],
        compiler_params=pltpu.CompilerParams(vmem_limit_bytes=58 * 1024 * 1024),
        cost_estimate=pl.CostEstimate(
            flops=2 * half * model_width * (heads.shape[1] + 5 * hidden_width),
            bytes_accessed=2 * (out_full.size + gate.size + up.size + down.size),
            transcendentals=half * hidden_width,
        ),
        name="feed_forward",
    )(rank, heads, tokens, grads, out_full, gain, gate, up, down, *earlier)


def small_sum(values, axis, size):
    total = values
    for shift in range(1, size):
        pairs = [(i, (i + shift) % size) for i in range(size)]
        total = total + lax.ppermute(values, axis, pairs)
    return total


def after(value, *others):
    return lax.optimization_barrier((value, others))[0]


def pair_sum(left, right, core, pairs):
    half = left.shape[1] // 2

    def rows(which):
        part = lax.dynamic_slice_in_dim(left, which * half, half, 1)
        return dot(part, right, ((0,), (0,)))

    received = lax.ppermute(rows(1 - core).astype(jnp.bfloat16), "dp", pairs)
    return (rows(core) + received.astype(jnp.float32)).astype(jnp.bfloat16)


def halving_sum(value, bits, rank, size, gates):
    for bit in bits:
        half = value.shape[0] // 2
        side = lax.rem(rank >> bit, 2)
        pairs = [(i, i ^ (1 << bit)) for i in range(size)]
        sent = lax.dynamic_slice_in_dim(value, (1 - side) * half, half, 0)
        kept = lax.dynamic_slice_in_dim(value, side * half, half, 0).astype(jnp.float32)
        value = (kept + lax.ppermute(sent, "dp", pairs).astype(jnp.float32)).astype(jnp.bfloat16)
    for place, bit in enumerate(reversed(bits)):
        value = after(value, gates[min(place, len(gates) - 1)])
        side = lax.rem(rank >> bit, 2)
        pairs = [(i, i ^ (1 << bit)) for i in range(size)]
        other = lax.ppermute(value, "dp", pairs)
        parts = (jnp.where(side == 0, value, other), jnp.where(side == 0, other, value))
        value = jnp.concatenate(parts, axis=0)
    return value


def chip_sum(value, rank, size, gates):
    bits = list(range(1, size.bit_length() - 1))
    half = value.shape[0] // 2
    parts = (
        halving_sum(value[:half], bits, rank, size, gates),
        halving_sum(value[half:], bits[::-1], rank, size, gates),
    )
    return jnp.concatenate(parts, axis=0)


def join_kernel(steps, core_ref, mine_ref, other_ref, *out_refs):
    own = (pl.program_id(0) < steps) == (core_ref[0] == 0)

    def write(source_ref):
        start = 0
        for out_ref in out_refs:
            width = out_ref.shape[1]
            out_ref[...] = source_ref[:, start : start + width].astype(jnp.float32)
            start += width

    pl.when(own)(lambda: write(mine_ref))
    pl.when(jnp.logical_not(own))(lambda: write(other_ref))


def both_halves(mine, core, pairs, widths):
    other = lax.ppermute(mine, "dp", pairs)
    half, width = mine.shape
    block = math.gcd(256, half)
    steps = half // block

    def place(step, first):
        return jnp.clip(step - jnp.where(first, 0, steps), 0, steps - 1)

    grid_spec = pltpu.PrefetchScalarGridSpec(
        num_scalar_prefetch=1,
        grid=(2 * steps,),
        in_specs=[
            pl.BlockSpec((block, width), lambda i, core_ref: (place(i, core_ref[0] == 0), 0)),
            pl.BlockSpec((block, width), lambda i, core_ref: (place(i, core_ref[0] != 0), 0)),
        ],
        out_specs=[pl.BlockSpec((block, each), lambda i, core_ref: (i, 0)) for each in widths],
    )
    return pl.pallas_call(
        partial(join_kernel, steps),
        grid_spec=grid_spec,
        out_shape=[jax.ShapeDtypeStruct((2 * half, each), jnp.float32) for each in widths],
        compiler_params=pltpu.CompilerParams(vmem_limit_bytes=32 * 1024 * 1024),
        cost_estimate=pl.CostEstimate(
            flops=mine.size, bytes_accessed=12 * mine.size, transcendentals=0
        ),
        name="join",
    )(core.astype(jnp.int32)[None], mine, other)


def local(
    tensor_size,
    dp_size,
    tokens,
    lengths,
    cotangent,
    first_gain,
    query_weight,
    key_weight,
    value_weight,
    query_gain,
    key_gain,
    out_weight,
    second_gain,
    gate_weight,
    up_weight,
    down_weight,
):
    bf16 = jnp.bfloat16
    tensor_rank = lax.axis_index("tensor")
    dp_rank = lax.axis_index("dp")
    seq_len = tokens.shape[0]
    share_width = tokens.shape[1]
    model_width = first_gain.shape[0]
    head_dim = query_gain.shape[0]
    local_heads = query_weight.shape[1] // head_dim
    local_groups = key_weight.shape[1] // head_dim
    length = lengths[0]
    valid_rows = (jnp.arange(seq_len, dtype=jnp.int32) < length).astype(jnp.float32)[:, None]
    own_start = tensor_rank * share_width
    first_own = lax.dynamic_slice_in_dim(first_gain, own_start, share_width, 0)
    second_own = lax.dynamic_slice_in_dim(second_gain, own_start, share_width, 0)
    full_tokens = lax.all_gather(tokens, "tensor", axis=1, tiled=True)
    out_cols = model_width // dp_size
    out_rows = out_weight.shape[0]
    out_part = lax.dynamic_slice_in_dim(out_weight, dp_rank * out_cols, out_cols, 1)
    pieces = [out_part]
    for shift in range(1, tensor_size):
        ring = [(i, (i + shift) % tensor_size) for i in range(tensor_size)]
        pieces.append(lax.ppermute(out_part, "tensor", ring))
    full_tokens = after(full_tokens, *pieces)
    full_cot = lax.all_gather(after(cotangent, full_tokens), "tensor", axis=1, tiled=True)
    out_block = jnp.zeros((out_rows * tensor_size, out_cols), bf16)
    for shift, piece in enumerate(pieces):
        source = lax.rem(tensor_rank + tensor_size - shift, tensor_size)
        out_block = lax.dynamic_update_slice_in_dim(out_block, piece, source * out_rows, 0)
    out_full = jnp.zeros((out_rows * tensor_size, model_width), bf16)
    out_full = lax.dynamic_update_slice_in_dim(out_full, out_block, dp_rank * out_cols, 1)
    rotated_order = [[(i + 1) % dp_size for i in range(dp_size)]]
    out_full = lax.psum(out_full, "dp", axis_index_groups=rotated_order)

    token_own = tokens.astype(jnp.float32)
    token_rows = full_tokens.astype(jnp.float32)
    first_root = lax.rsqrt(jnp.mean(token_rows * token_rows, axis=1, keepdims=True) + EPSILON)
    normed = (token_rows * first_root * first_gain).astype(bf16)
    heads_weight = jnp.concatenate([query_weight, key_weight, value_weight], axis=1)
    raw = dot(normed, heads_weight, ((1,), (0,)))
    cosine, sine = rope_rows(seq_len, head_dim)
    head_gains = (query_gain[None, :], key_gain[None, :])
    counts = (local_heads, local_groups)
    attended, query_rows, key_rows = attention(lengths, raw, *head_gains, cosine, sine, *counts)

    out_full = after(out_full, attended)
    attended = after(attended, full_cot)
    grad_full = (full_cot.astype(jnp.float32) * valid_rows).astype(bf16)
    grad_own = cotangent.astype(jnp.float32) * valid_rows
    out_full = after(out_full, grad_full)

    half = seq_len // 2
    heads_in = (attended[:half], after(attended[half:], grad_full))
    heads_parts = [lax.all_gather(part, "tensor", axis=1, tiled=True) for part in heads_in]
    rank = tensor_rank.astype(jnp.int32)[None]
    grad_parts, mid_parts, kept = [], [], []
    for part, heads_full in enumerate(heads_parts):
        *kept, mid, mixed_grad = feed_forward(
            part,
            kept,
            rank,
            heads_full,
            full_tokens,
            grad_full,
            out_full,
            second_gain[None, :],
            gate_weight,
            up_weight,
            down_weight,
            share_width,
        )
        mid_parts.append(mid[:, 0])
        if grad_parts:
            mixed_grad = after(mixed_grad, grad_parts[-1])
        grad_parts.append(lax.psum_scatter(mixed_grad, "tensor", scatter_dimension=1, tiled=True))
    mixed_rows, product, gate_grads, up_grads, hidden_own, second_root = kept
    core = lax.rem(dp_rank, 2)
    pairs = [(i, i ^ 1) for i in range(dp_size)]
    chips = [[i for i in range(dp_size) if i % 2 == side] for side in (0, 1)]
    early = (
        pair_sum(product, grad_full, core, pairs),
        pair_sum(mixed_rows, gate_grads, core, pairs),
        pair_sum(mixed_rows, up_grads, core, pairs),
    )
    down_part = dot(after(product, *early), down_weight, ((1,), (0,))).astype(bf16)
    mid_total = small_sum(jnp.concatenate(mid_parts), "tensor", tensor_size)[:, None]
    grad_parts, mid_total = after((grad_parts, mid_total), *early)
    mixed_own_grad = jnp.concatenate(grad_parts, axis=0).astype(jnp.float32)
    early = lax.psum(early, "dp", axis_index_groups=chips)

    second_gain_grad = jnp.sum(mixed_own_grad * hidden_own * second_root, axis=0)
    hidden_grad = (
        grad_own
        + mixed_own_grad * second_own * second_root
        - hidden_own * second_root**2 / model_width * mid_total
    )
    hidden_grad_rows = lax.all_gather(hidden_grad.astype(bf16), "tensor", axis=1, tiled=True)
    down_part, hidden_grad_rows = lax.optimization_barrier((down_part, hidden_grad_rows))
    down_own = lax.psum_scatter(down_part, "tensor", scatter_dimension=1, tiled=True)
    attended_grad = dot(hidden_grad_rows, out_weight, ((1,), (1,))).astype(bf16)
    *raw_grads, query_gain_grad, key_gain_grad, row_sum = attention_back(
        lengths, query_rows, key_rows, raw, attended_grad, *head_gains, cosine, sine, *counts
    )
    raw_grad = jnp.concatenate(raw_grads, axis=1)
    row_sum = small_sum(row_sum[:, 0], "tensor", tensor_size)[:, None]
    normed_grad = dot(raw_grad, heads_weight, ((1,), (1,))).astype(bf16)
    normed_own_grad = lax.psum_scatter(normed_grad, "tensor", scatter_dimension=1, tiled=True)
    first_gain_part = jnp.sum(
        normed_grad.astype(jnp.float32) * (full_tokens.astype(jnp.float32) * first_root), axis=0
    )
    second_gain_part = lax.dynamic_update_slice_in_dim(
        jnp.zeros((model_width,), jnp.float32), second_gain_grad, own_start, 0
    )
    gains = [first_gain_part, second_gain_part, query_gain_grad[0], key_gain_grad[0]]
    gains = small_sum(jnp.concatenate(gains), "tensor", tensor_size)
    for bit in range(dp_size.bit_length() - 1):
        gains = gains + lax.ppermute(gains, "dp", [(i, i ^ (1 << bit)) for i in range(dp_size)])
    grad_out = pair_sum(attended, hidden_grad_rows, core, pairs)
    grad_heads = pair_sum(normed, raw_grad, core, pairs)
    early = after(early, grad_out, grad_heads, gains, row_sum)
    down_own = after(down_own, normed_grad, grad_out, grad_heads)
    (grad_down,), (grad_gate,), (grad_up,) = (
        both_halves(part, core, pairs, (part.shape[1],)) for part in early
    )
    gates = (early, grad_down)
    grad_out, grad_heads = (
        chip_sum(after(part, normed_grad), dp_rank, dp_size, gates)
        for part in (grad_out, grad_heads)
    )
    layer_out = (hidden_own + down_own.astype(jnp.float32)).astype(bf16)
    normed_own_grad = after(normed_own_grad, layer_out, gains, *early).astype(jnp.float32)
    token_grad = (
        hidden_grad
        + normed_own_grad * first_own * first_root
        - token_own * first_root**2 / model_width * row_sum
    ).astype(bf16)
    grad_out, grad_heads = after(
        (grad_out, grad_heads), grad_gate, grad_up, layer_out, token_grad
    )
    (grad_out,) = both_halves(grad_out, core, pairs, (model_width,))
    query_width, key_width = query_weight.shape[1], key_weight.shape[1]
    grad_query, grad_key, grad_value = both_halves(
        grad_heads, core, pairs, (query_width, key_width, key_width)
    )
    first_gain_grad = lax.dynamic_slice_in_dim(gains, own_start, share_width, 0)
    second_gain_grad = lax.dynamic_slice_in_dim(gains, model_width + own_start, share_width, 0)
    query_gain_grad = gains[2 * model_width : 2 * model_width + head_dim]
    key_gain_grad = gains[2 * model_width + head_dim :]
    return (
        layer_out,
        token_grad,
        first_gain_grad,
        grad_query,
        grad_key,
        grad_value,
        query_gain_grad,
        key_gain_grad,
        grad_out,
        second_gain_grad,
        grad_gate,
        grad_up,
        grad_down,
    )


def solution(mesh):
    in_specs = (
        P("dp", "tensor"),
        P("dp"),
        P("dp", "tensor"),
        P(),
        P(None, "tensor"),
        P(None, "tensor"),
        P(None, "tensor"),
        P(),
        P(),
        P("tensor", None),
        P(),
        P(None, "tensor"),
        P(None, "tensor"),
        P("tensor", None),
    )
    out_specs = (
        P("dp", "tensor"),
        P("dp", "tensor"),
        P("tensor"),
        P(None, "tensor"),
        P(None, "tensor"),
        P(None, "tensor"),
        P(),
        P(),
        P("tensor", None),
        P("tensor"),
        P(None, "tensor"),
        P(None, "tensor"),
        P("tensor", None),
    )
    return jax.shard_map(
        partial(local, mesh.shape["tensor"], mesh.shape["dp"]), mesh=mesh, in_specs=in_specs, out_specs=out_specs, check_vma=False)
```
